32 devices in a mesh: ctx: 8 (over z, x), fsdp: 4 (over y, core).
Axes of the slice: x: 2, y: 2, z: 4, core: 2. Of those that a mesh axis runs over, the one named last changes fastest.
Arguments:
- inputs: bfloat16 [5120, 2304], P(('ctx', 'fsdp')), may hold values from -6 to 6
- cotangent: bfloat16 [5120, 2304], P(('ctx', 'fsdp')), may hold values from -6 to 6
- w_query: bfloat16 [2304, 2048], P(('ctx', 'fsdp')), may hold values from -0.25 to 0.25
- w_key: bfloat16 [2304, 1024], P(('ctx', 'fsdp')), may hold values from -0.125 to 0.125
- w_value: bfloat16 [2304, 1024], P(('ctx', 'fsdp')), may hold values from -0.125 to 0.125
- w_out_t: bfloat16 [2304, 2048], P(('ctx', 'fsdp')), may hold values from -0.125 to 0.125
- w_gate: bfloat16 [2304, 9216], P(('ctx', 'fsdp')), may hold values from -0.125 to 0.125
- w_up: bfloat16 [2304, 9216], P(('ctx', 'fsdp')), may hold values from -0.125 to 0.125
- w_down_t: bfloat16 [2304, 9216], P(('ctx', 'fsdp')), may hold values from -0.0625 to 0.0625
- gain_attn_in: bfloat16 [2304], P(('ctx', 'fsdp')), may hold values from 0.25 to 1.75
- gain_attn_out: bfloat16 [2304], P(('ctx', 'fsdp')), may hold values from 0.25 to 1.75
- gain_mlp_in: bfloat16 [2304], P(('ctx', 'fsdp')), may hold values from 0.25 to 1.75
- gain_mlp_out: bfloat16 [2304], P(('ctx', 'fsdp')), may hold values from 0.25 to 1.75
Outputs:
- output: bfloat16 [5120, 2304], P(('ctx', 'fsdp'))
- input_grad: bfloat16 [5120, 2304], P(('ctx', 'fsdp'))
- grad_query: float32 [2304, 2048], P(('ctx', 'fsdp'))
- grad_key: float32 [2304, 1024], P(('ctx', 'fsdp'))
- grad_value: float32 [2304, 1024], P(('ctx', 'fsdp'))
- grad_out_t: float32 [2304, 2048], P(('ctx', 'fsdp'))
- grad_gate: float32 [2304, 9216], P(('ctx', 'fsdp'))
- grad_up: float32 [2304, 9216], P(('ctx', 'fsdp'))
- grad_down_t: float32 [2304, 9216], P(('ctx', 'fsdp'))
- grad_gain_attn_in: float32 [2304], P(('ctx', 'fsdp'))
- grad_gain_attn_out: float32 [2304], P(('ctx', 'fsdp'))
- grad_gain_mlp_in: float32 [2304], P(('ctx', 'fsdp'))
- grad_gain_mlp_out: float32 [2304], P(('ctx', 'fsdp'))
The draws below stay inside these ranges and needn't reach their ends.
All inputs are finite; a program needn't handle non-finite values.
Results may differ from the reference program's by a relative error of at most 0.023.
Values may be sent and summed in bfloat16 or wider, within the bound.
No kernel may reach another device: no remote copies, remote signals or barrier semaphores. Data moves between devices by JAX's collectives and lax.ppermute only.
A program may use at most 320 MiB of HBM per device.

```python
import jax
import jax.numpy as jnp
from jax import lax

D = 2304
HEADS = 8
KV_HEADS = 4
HEAD = 256
FF = 9216
WINDOW = 4096
CAP = 10
TOK_DEV = 160
TOKENS = 5120
N_CTX = 8
N_FSDP = 4


def shard_levels(rng, dims, pieces, low, largest):
    gain = 1.0
    for dim, parts in pieces:
        heights = jax.random.uniform(jax.random.fold_in(jax.random.fold_in(rng, 6), dim), (parts,), jnp.float32, low / len(pieces), largest / len(pieces))
        gain = gain * jnp.repeat(jnp.exp(heights), dims[dim] // parts).reshape((-1,) + (1,) * (len(dims) - 1 - dim))
    return gain


def scatter_about(own_key, extent, width, reach, split=(), kind=jnp.bfloat16):
    factor_of = shard_levels(own_key, extent, split, -0.22, 0.18) if split else 1.0
    values = jax.random.normal(own_key, extent, jnp.float32) * width * factor_of
    return jnp.minimum(jnp.maximum(values, -reach), reach).astype(kind)


def setup_inputs(seed: int = 0) -> dict:
    key_of = jax.random.split(jax.random.key(seed), 14)
    return {
        "inputs": scatter_about(key_of[0], (TOKENS, D), 1.0, 6.0, ((0, 32),)),
        "cotangent": scatter_about(key_of[1], (TOKENS, D), 1.0, 6.0, ((0, 32),)),
        "w_query": scatter_about(key_of[2], (D, HEADS * HEAD), (D // 4) ** -0.5, 0.25, ((0, 32),)),
        "w_key": scatter_about(key_of[3], (D, KV_HEADS * HEAD), D ** -0.5, 0.125, ((0, 32),)),
        "w_value": scatter_about(key_of[4], (D, KV_HEADS * HEAD), D ** -0.5, 0.125, ((0, 32),)),
        "w_out_t": scatter_about(key_of[5], (D, HEADS * HEAD), (HEADS * HEAD) ** -0.5, 0.125, ((0, 32),)),
        "w_gate": scatter_about(key_of[6], (D, FF), D ** -0.5, 0.125, ((0, 32),)),
        "w_up": scatter_about(key_of[7], (D, FF), D ** -0.5, 0.125, ((0, 32),)),
        "w_down_t": scatter_about(key_of[8], (D, FF), FF ** -0.5, 0.0625, ((0, 32),)),
        "gain_attn_in": jnp.clip(1.0 + 0.15 * jax.random.normal(key_of[9], (D,), jnp.float32), 0.25, 1.75).astype(jnp.bfloat16),
        "gain_attn_out": jnp.clip(1.0 + 0.15 * jax.random.normal(key_of[10], (D,), jnp.float32), 0.25, 1.75).astype(jnp.bfloat16),
        "gain_mlp_in": jnp.clip(1.0 + 0.15 * jax.random.normal(key_of[11], (D,), jnp.float32), 0.25, 1.75).astype(jnp.bfloat16),
        "gain_mlp_out": jnp.clip(1.0 + 0.15 * jax.random.normal(key_of[12], (D,), jnp.float32), 0.25, 1.75).astype(jnp.bfloat16),
    }


@jax.custom_vjp
def low(v):
    return lax.optimization_barrier(v.astype(jnp.bfloat16)).astype(jnp.float32)

@jax.custom_vjp
def low_back(v):
    return v

def low_keep(v):
    return (low(v), None)

def low_pass(kept, grad):
    return (grad,)

def back_keep(v):
    return (v, None)

def back_low(kept, grad):
    return (low(grad),)
low.defvjp(low_keep, low_pass)
low_back.defvjp(back_keep, back_low)
epsilon = 1e-06
masked_value = -1e+30

def matmul(left_side, right_side):
    return jnp.dot(left_side, right_side, precision=lax.Precision.HIGHEST)

def normed(values, weights):
    scaling = lax.rsqrt(lax.optimization_barrier(jnp.mean(values * values, axis=-1, keepdims=True)) + epsilon)
    return values * scaling * weights

def rotary(values, positions):
    halfway = values.shape[-1] // 2
    frequency = 10000.0 ** (-jnp.arange(halfway, dtype=jnp.float32) * 2.0 / values.shape[-1])
    angles = positions.astype(jnp.float32)[:, None] * frequency[None, :]
    cosine = jnp.cos(angles)[:, None, :]
    sine_value = jnp.sin(angles)[:, None, :]
    leading = values[..., :halfway]
    trailing = values[..., halfway:]
    return jnp.concatenate([leading * cosine - trailing * sine_value, trailing * cosine + leading * sine_value], axis=-1)

def attention(query, keyed, valued):
    block_len = TOK_DEV * N_FSDP
    reach_blocks = (WINDOW + block_len - 2) // block_len
    group_size = HEADS // KV_HEADS
    span_len = (reach_blocks + 1) * block_len
    padding = jnp.zeros((reach_blocks * block_len, KV_HEADS, HEAD), jnp.float32)
    keys_padded = jnp.concatenate([padding, keyed], axis=0)
    values_padded = jnp.concatenate([padding, valued], axis=0)
    query_blocks = query.reshape(N_CTX, block_len, KV_HEADS, group_size, HEAD)

    @jax.checkpoint
    def one_block(query_block, block_index, keys_all, values_all):
        begin = (block_index * block_len).astype(jnp.int32)
        key_window = lax.dynamic_slice_in_dim(keys_all, begin, span_len, 0)
        value_window = lax.dynamic_slice_in_dim(values_all, begin, span_len, 0)
        query_pos = block_index * block_len + jnp.arange(block_len, dtype=jnp.int32)
        key_pos = (block_index - reach_blocks) * block_len + jnp.arange(span_len, dtype=jnp.int32)
        allowed = (key_pos[None, :] <= query_pos[:, None]) & (query_pos[:, None] - key_pos[None, :] < WINDOW) & (key_pos[None, :] >= 0)
        raw_scores = low_back(jnp.einsum('rhgd,khd->hgrk', query_block, key_window, precision=lax.Precision.HIGHEST) * HEAD ** (-0.5))
        capped = CAP * jnp.tanh(raw_scores / CAP)
        masked = jnp.where(allowed[None, None], capped, masked_value)
        probabilities = low(jax.nn.softmax(masked, axis=-1))
        return jnp.einsum('hgrk,khd->rhgd', probabilities, value_window, precision=lax.Precision.HIGHEST)

    def run_block(entries):
        return one_block(entries[0], entries[1], keys_padded, values_padded)
    results = lax.map(run_block, (query_blocks, jnp.arange(N_CTX, dtype=jnp.int32)))
    return results.reshape(TOKENS, HEADS * HEAD)

def layer(source, w_query, w_key, w_value, w_out_t, w_gate, w_up, w_down_t, gain_attn_in, gain_attn_out, gain_mlp_in, gain_mlp_out):
    positions = jnp.arange(TOKENS, dtype=jnp.int32)
    attn_in = low(normed(source, gain_attn_in))
    query = low(rotary(low_back(matmul(attn_in, w_query)).reshape(TOKENS, HEADS, HEAD), positions))
    keyed = low(rotary(low_back(matmul(attn_in, w_key)).reshape(TOKENS, KV_HEADS, HEAD), positions))
    valued = low(low_back(matmul(attn_in, w_value))).reshape(TOKENS, KV_HEADS, HEAD)
    attended = low(low_back(attention(query, keyed, valued)))
    projected = low_back(matmul(attended, w_out_t.T))
    hidden = source + normed(projected, gain_attn_out)
    mlp_in = low(normed(hidden, gain_mlp_in))
    gate_val = low(low_back(matmul(mlp_in, w_gate)))
    up_val = low(low_back(matmul(mlp_in, w_up)))
    mixed = low(jax.nn.gelu(gate_val, approximate=True) * up_val)
    reduced = low_back(matmul(mixed, w_down_t.T))
    return hidden + normed(reduced, gain_mlp_out)

def reference(inputs, cotangent, w_query, w_key, w_value, w_out_t, w_gate, w_up, w_down_t, gain_attn_in, gain_attn_out, gain_mlp_in, gain_mlp_out):
    floats = [array_in.astype(jnp.float32) for array_in in (inputs, w_query, w_key, w_value, w_out_t, w_gate, w_up, w_down_t, gain_attn_in, gain_attn_out, gain_mlp_in, gain_mlp_out)]
    result, pullback = jax.vjp(layer, *floats)
    grads = pullback(cotangent.astype(jnp.float32))
    return (result.astype(jnp.bfloat16), grads[0].astype(jnp.bfloat16), grads[1], grads[2], grads[3], grads[4], grads[5], grads[6], grads[7], grads[8], grads[9], grads[10], grads[11])
```

```python
import jax
import jax.numpy as jnp
from jax import lax
from jax.experimental import pallas as pl
from jax.experimental.pallas import tpu as pltpu
from jax.sharding import Mesh
from jax.sharding import PartitionSpec as P

HEADS = 8
KV_HEADS = 4
HEAD = 256
WINDOW = 4096
CAP = 10.0
EPS = 1e-06
SCALE = HEAD**-0.5
BLOCK = 256

RING = 4
AXES = ("z", "b", "y", "c")
GROUP = ("z", "c")
COPIES = ("b", "y")

bf16 = jnp.bfloat16
f32 = jnp.float32


def swapped(value, axis):
    return lax.ppermute(value, axis, [(0, 1), (1, 0)])


def rotated(value, axis, steps):
    count = lax.axis_size(axis)
    return lax.ppermute(value, axis, [(i, (i + steps) % count) for i in range(count)])


def join(*values):
    return lax.optimization_barrier(values)


def dot_nn(left, right):
    return lax.dot_general(left, right, (((1,), (0,)), ((), ())), preferred_element_type=f32)


def dot_nt(left, right):
    return lax.dot_general(left, right, (((1,), (1,)), ((), ())), preferred_element_type=f32)


def dot_tn(left, right):
    return lax.dot_general(left, right, (((0,), (0,)), ((), ())), preferred_element_type=f32)


def moved(values, first, second):
    rest = values.shape[1] // (first * second)
    starts = [(i * second + j) * rest for j in range(second) for i in range(first)]
    return jnp.concatenate([values[:, s : s + rest] for s in starts], axis=1)


def copies_first(values, normed=False):
    rows, width = values.shape
    copies = lax.axis_size("b") * lax.axis_size("y")

    def kernel(in_ref, out_ref, *normed_refs):
        here = moved(in_ref[...].astype(f32), RING, copies)
        out_ref[...] = here.astype(out_ref.dtype)
        if normed:
            inverse = lax.rsqrt(jnp.mean(here * here, axis=1, keepdims=True) + EPS)
            normed_refs[0][...] = (here * inverse).astype(bf16)
            normed_refs[1][...] = inverse

    out_shape = [jax.ShapeDtypeStruct((rows, width), values.dtype)]
    if normed:
        out_shape.append(jax.ShapeDtypeStruct((rows, width), bf16))
        out_shape.append(jax.ShapeDtypeStruct((rows, 1), f32))
    result = pl.pallas_call(
        kernel,
        out_shape=out_shape,
        compiler_params=pltpu.CompilerParams(vmem_limit_bytes=24 << 20),
        cost_estimate=pl.CostEstimate(
            flops=rows * width, bytes_accessed=8 * rows * width, transcendentals=0
        ),
        name="copies_first",
    )(values)
    return result if normed else result[0]


def copies_back(values):
    rows, width = values.shape
    copies = lax.axis_size("b") * lax.axis_size("y")

    def kernel(in_ref, out_ref):
        out_ref[...] = moved(in_ref[...].astype(f32), copies, RING).astype(out_ref.dtype)

    return pl.pallas_call(
        kernel,
        out_shape=jax.ShapeDtypeStruct((rows, width), values.dtype),
        compiler_params=pltpu.CompilerParams(vmem_limit_bytes=24 << 20),
        cost_estimate=pl.CostEstimate(
            flops=rows * width, bytes_accessed=8 * rows * width, transcendentals=0
        ),
        name="copies_back",
    )(values)


def gather_tokens(own, work=None, beside=(None, None, None)):
    half = own.shape[0] // 2
    up, down = own[:half], own[half:]
    chunks, results = [jnp.concatenate([own, swapped(own, "c")], axis=0)], []
    beside = list(beside)
    for step in range(RING):
        results.append(work(step, chunks[step]) if work else ())
        if step == RING - 1:
            return chunks, results, beside
        up, down = rotated(up, "z", 1), rotated(down, "z", -1)
        extra = beside[step] or ()
        if results[step] or extra:
            up, down, results[step], beside[step] = join(up, down, results[step], extra)
        both = jnp.concatenate([up, down], axis=0)
        chunks.append(jnp.concatenate([both, swapped(both, "c")], axis=0))


def relative_places():
    place = None
    for axis in AXES:
        count = lax.axis_size(axis)
        at = (lax.axis_index(axis) - jnp.arange(count, dtype=jnp.int32)) % count
        place = at if place is None else (place[:, None] * count + at[None, :]).reshape(-1)
    return place


def gather_small(value):
    for axis in AXES[::-1]:
        parts = [value] + [rotated(value, axis, k) for k in range(1, lax.axis_size(axis))]
        value = jnp.concatenate(parts, axis=0)
    place = relative_places()
    chosen = place[None, :] == jnp.arange(place.shape[0], dtype=jnp.int32)[:, None]
    return dot_nn(chosen.astype(value.dtype), value)


def scatter_small(value):
    place = relative_places()
    chosen = place[:, None] == jnp.arange(place.shape[0], dtype=jnp.int32)[None, :]
    value = jnp.dot(
        chosen.astype(f32), value, precision=lax.Precision.HIGHEST, preferred_element_type=f32
    )
    for axis in AXES:
        count = lax.axis_size(axis)
        parts = value.reshape(count, -1, value.shape[1])
        total = parts[0]
        for k in range(1, count):
            total = total + rotated(parts[k], axis, -k)
        value = total
    return value[0]


def scatter_tokens(chunks, beside=(None, None, None)):
    rows = chunks[0].shape[0] // 2
    half = rows // 2
    carried = None
    beside = list(beside)
    for step in range(RING):
        chunk = chunks[(step + 1) % RING]
        here = chunk[:rows].astype(f32) + swapped(chunk[rows:], "c").astype(f32)
        if carried is not None:
            here = here + carried.astype(f32)
        if step == RING - 1:
            return here, beside
        sent = here.astype(bf16)
        up, down = rotated(sent[:half], "z", 1), rotated(sent[half:], "z", -1)
        if beside[step] is not None:
            up, down, *beside[step] = join(up, down, *beside[step])
        carried = jnp.concatenate([up, down], axis=0)


def ring_pieces(values, tok):
    half = tok // 2
    return values.reshape(RING, 2, 2, half, values.shape[-1])


def by_block(values, tok):
    parts = ring_pieces(values, tok)
    order = [0] + list(range(RING - 1, 0, -1))
    blocks = [jnp.stack([parts[i, :, 0], parts[order[i], :, 1]], axis=1) for i in range(RING)]
    return jnp.concatenate([block.reshape(2 * tok, -1) for block in blocks], axis=0)


def exchange(blocks):
    return lax.all_to_all(blocks, GROUP, split_axis=0, concat_axis=0, tiled=True)


def gather_rows(blocks):
    parts, rows, cols = blocks.shape
    return lax.all_gather(blocks.reshape(parts * rows, cols), COPIES, axis=0, tiled=True)


def scatter_rows(grad):
    total = lax.psum_scatter(grad, COPIES, scatter_dimension=0, tiled=True)
    return total.reshape(8, -1, grad.shape[1])


def split_cols(weight):
    rows, cols = weight.shape
    return weight.reshape(rows, 8, cols // 8).transpose(1, 0, 2)


def join_cols(blocks):
    parts, rows, cols = blocks.shape
    return blocks.transpose(1, 0, 2).reshape(rows, parts * cols)


def attention_forward(q, kv, meta, q_pos, k_pos, q_block):
    tokens = q.shape[0]
    keys = kv.shape[1]
    steps = tokens // q_block
    key_steps = keys // BLOCK

    def kernel(meta_ref, q_ref, kv_ref, q_pos_ref, k_pos_ref, o_ref, lse_ref, acc_ref, sum_ref):
        i = pl.program_id(0)
        core = meta_ref[0]
        q_low, q_high = meta_ref[1 + 2 * i], meta_ref[2 + 2 * i]
        acc_ref[...] = jnp.zeros_like(acc_ref)
        sum_ref[...] = jnp.zeros_like(sum_ref)

        def step(j, carry):
            k_low = meta_ref[1 + 2 * steps + 2 * j]
            k_high = meta_ref[2 + 2 * steps + 2 * j]

            @pl.when((q_high >= k_low) & (q_low - k_high < WINDOW))
            def _():
                place = pl.ds(pl.multiple_of(j * BLOCK, BLOCK), BLOCK)
                key = kv_ref[core, place, :]
                value = kv_ref[1 - core, place, :]
                scores = dot_nt(q_ref[...], key)
                turned = jnp.tanh(scores * (SCALE / CAP))
                away = q_pos_ref[...] - k_pos_ref[j]
                weight = jnp.where((away >= 0) & (away < WINDOW), jnp.exp(turned * CAP), 0.0)
                sum_ref[...] += jnp.sum(weight, axis=1, keepdims=True)
                acc_ref[...] += dot_nn(weight.astype(bf16), value)

            return carry

        lax.fori_loop(0, key_steps, step, 0)
        total = sum_ref[...]
        o_ref[...] = acc_ref[...] / total
        lse_ref[...] = jnp.log(total)

    return pl.pallas_call(
        kernel,
        grid=(steps,),
        in_specs=[
            pl.BlockSpec(memory_space=pltpu.SMEM),
            pl.BlockSpec((q_block, HEAD), lambda i: (i, 0)),
            pl.BlockSpec(memory_space=pltpu.VMEM),
            pl.BlockSpec((q_block, 1), lambda i: (i, 0)),
            pl.BlockSpec(memory_space=pltpu.VMEM),
        ],
        out_specs=[
            pl.BlockSpec((q_block, HEAD), lambda i: (i, 0)),
            pl.BlockSpec((q_block, 1), lambda i: (i, 0)),
        ],
        out_shape=[
            jax.ShapeDtypeStruct((tokens, HEAD), f32),
            jax.ShapeDtypeStruct((tokens, 1), f32),
        ],
        scratch_shapes=[pltpu.VMEM((q_block, HEAD), f32), pltpu.VMEM((q_block, 1), f32)],
        compiler_params=pltpu.CompilerParams(vmem_limit_bytes=2 * kv.size + (12 << 20)),
        cost_estimate=pl.CostEstimate(
            flops=4 * tokens * keys * HEAD,
            bytes_accessed=2 * kv.size + 8 * tokens * HEAD,
            transcendentals=2 * tokens * keys,
        ),
        name="attention_forward",
    )(meta, q, kv, q_pos, k_pos)


def attention_backward(q, d_out, kv, meta, lse, delta, q_pos, k_pos):
    tokens = q.shape[0]
    keys = kv.shape[1]
    steps = tokens // BLOCK
    key_steps = keys // BLOCK

    def kernel(
        meta_ref, q_ref, d_ref, kv_ref, lse_ref, delta_ref, q_pos_ref, k_pos_ref,
        dq_ref, dkv_ref, key_acc, value_acc,
    ):
        j = pl.program_id(0)
        core = meta_ref[0]
        k_low = meta_ref[1 + 2 * steps + 2 * j]
        k_high = meta_ref[2 + 2 * steps + 2 * j]

        @pl.when(j == 0)
        def _():
            dq_ref[...] = jnp.zeros_like(dq_ref)

        key_acc[...] = jnp.zeros_like(key_acc)
        value_acc[...] = jnp.zeros_like(value_acc)
        for i in range(steps):
            q_low, q_high = meta_ref[1 + 2 * i], meta_ref[2 + 2 * i]

            @pl.when((q_high >= k_low) & (q_low - k_high < WINDOW))
            def _(i=i):
                place = pl.ds(i * BLOCK, BLOCK)
                key = kv_ref[core]
                value = kv_ref[1 - core]
                query = q_ref[place, :]
                d_here = d_ref[place, :]
                turned = jnp.tanh(dot_nt(key, query) * (SCALE / CAP))
                away = q_pos_ref[:, place] - k_pos_ref[...]
                soft = jnp.where(
                    (away >= 0) & (away < WINDOW),
                    jnp.exp(turned * CAP - lse_ref[:, place]),
                    0.0,
                )
                d_prob = dot_nt(value, d_here)
                d_raw = soft * (d_prob - delta_ref[:, place]) * (1.0 - turned * turned)
                d_raw = d_raw.astype(bf16)
                value_acc[...] += dot_nn(soft.astype(bf16), d_here)
                key_acc[...] += dot_nn(d_raw, query)
                dq_ref[place, :] += dot_tn(d_raw, key)

        dkv_ref[core] = (key_acc[...] * SCALE).astype(bf16)
        dkv_ref[1 - core] = value_acc[...].astype(bf16)

        @pl.when(j == key_steps - 1)
        def _():
            dq_ref[...] = dq_ref[...] * SCALE

    whole = pl.BlockSpec(memory_space=pltpu.VMEM)
    return pl.pallas_call(
        kernel,
        grid=(key_steps,),
        in_specs=[
            pl.BlockSpec(memory_space=pltpu.SMEM),
            whole,
            whole,
            pl.BlockSpec((2, BLOCK, HEAD), lambda j: (0, j, 0)),
            whole,
            whole,
            whole,
            pl.BlockSpec((BLOCK, 1), lambda j: (j, 0)),
        ],
        out_specs=[whole, pl.BlockSpec((2, BLOCK, HEAD), lambda j: (0, j, 0))],
        out_shape=[
            jax.ShapeDtypeStruct((tokens, HEAD), f32),
            jax.ShapeDtypeStruct((2, keys, HEAD), bf16),
        ],
        scratch_shapes=[pltpu.VMEM((BLOCK, HEAD), f32), pltpu.VMEM((BLOCK, HEAD), f32)],
        compiler_params=pltpu.CompilerParams(vmem_limit_bytes=24 << 20),
        cost_estimate=pl.CostEstimate(
            flops=10 * tokens * keys * HEAD,
            bytes_accessed=4 * kv.size + 8 * tokens * HEAD,
            transcendentals=2 * tokens * keys,
        ),
        name="attention_backward",
    )(meta, q, d_out, kv, lse, delta, q_pos, k_pos)


def turn(values, cosine, sine):
    half = HEAD // 2
    parts = []
    for first in range(0, values.shape[1], HEAD):
        i = first // HEAD
        a = values[:, first : first + half]
        b = values[:, first + half : first + HEAD]
        parts += [a * cosine[i] - b * sine[i], b * cosine[i] + a * sine[i]]
    return jnp.concatenate(parts, axis=1)


def mean(values):
    return jnp.mean(values, axis=1, keepdims=True)


def gelu_parts(u):
    k = 0.7978845608028654
    t = jnp.tanh(k * (u + 0.044715 * u * u * u))
    value = 0.5 * u * (1.0 + t)
    slope = 0.5 * (1.0 + t) + 0.5 * u * (1.0 - t * t) * k * (1.0 + 3 * 0.044715 * u * u)
    return value, slope


def body(
    inputs,
    cotangent,
    w_query,
    w_key,
    w_value,
    w_out_t,
    w_gate,
    w_up,
    w_down_t,
    gain_attn_in,
    gain_attn_out,
    gain_mlp_in,
    gain_mlp_out,
):
    tok, width = inputs.shape
    rows = w_query.shape[0]
    count_b, count_y = lax.axis_size("b"), lax.axis_size("y")
    z, b, y, c = [lax.axis_index(name) for name in AXES]

    g_attn = gain_attn_in.astype(f32)[:, None]
    g_mlp = gain_mlp_in.astype(f32)[:, None]

    def scaled(weight, gain):
        return (weight.astype(f32) * gain).astype(bf16)

    pairs = jnp.stack(
        [w_key.reshape(rows, KV_HEADS, HEAD), w_value.reshape(rows, KV_HEADS, HEAD)], axis=2
    ).reshape(rows, 8, HEAD)
    qkv_pack = jnp.concatenate([w_query.reshape(rows, 8, HEAD), pairs], axis=2)
    qkv_pack = (qkv_pack.astype(f32) * g_attn[:, :, None]).astype(bf16).transpose(1, 0, 2)
    x, normed_x, r1 = copies_first(inputs, normed=True)
    x = x.astype(f32)
    out_pack = split_cols(w_out_t)
    gate_pack = split_cols(scaled(w_gate, g_mlp))
    up_pack = split_cols(scaled(w_up, g_mlp))
    down_pack = split_cols(w_down_t)
    qkv_w = gather_rows(exchange(qkv_pack))
    gains = jnp.concatenate([gain_attn_out, gain_mlp_out])[None]
    gains = gather_small(gains)
    x1, _, ((out_pack,), _, _) = gather_tokens(normed_x, None, ((out_pack,), None, None))
    out_mine = exchange(out_pack)
    x1[3], out_mine, gate_pack, gains = join(x1[3], out_mine, gate_pack, gains)
    out_w = gather_rows(out_mine)
    gate_mine = exchange(gate_pack)
    qkv = jnp.concatenate([dot_nn(part, qkv_w) for part in x1], axis=0)
    g_attn_out = moved(gains[:, :rows].reshape(1, width), RING, count_b * count_y)
    g_mlp_out = moved(gains[:, rows:].reshape(1, width), RING, count_b * count_y)

    def positions(places_b, places_y, places_c):
        blocks = (z - jnp.arange(RING, dtype=jnp.int32)) % RING
        place = (blocks * count_b + places_b[:, None, None]) * count_y + places_y[:, None]
        place = place[..., None] * 2 + places_c
        place = place[..., None] * tok + jnp.arange(tok, dtype=jnp.int32)
        return place.reshape(-1)

    cores = jnp.arange(2, dtype=jnp.int32)
    q_pos = positions(b[None], y[None], c ^ cores)
    k_pos = positions(
        (b - jnp.arange(count_b, dtype=jnp.int32)) % count_b,
        (y - jnp.arange(count_y, dtype=jnp.int32)) % count_y,
        cores,
    )

    def by_core(values):
        parts = values.reshape(RING, 2, tok, HEAD)
        return jnp.where(c == 0, parts, parts[:, ::-1]).reshape(values.shape)

    def bounds(places, block):
        blocks = places.reshape(-1, block)
        return jnp.stack([jnp.min(blocks, axis=1), jnp.max(blocks, axis=1)], axis=1).reshape(-1)

    q_block = 2 * tok
    core_id = c.astype(jnp.int32)[None]
    meta_forward = jnp.concatenate([core_id, bounds(q_pos, q_block), bounds(k_pos, BLOCK)])
    meta_backward = jnp.concatenate([core_id, bounds(q_pos, BLOCK), bounds(k_pos, BLOCK)])
    frequency = 10000.0 ** (-jnp.arange(HEAD // 2, dtype=f32) * 2.0 / HEAD)
    angles = q_pos.astype(f32)[:, None] * frequency[None, :]
    cos_q, sin_q = jnp.cos(angles), jnp.sin(angles)
    cos_kv, sin_kv = jnp.where(c == 0, cos_q, 1.0), jnp.where(c == 0, sin_q, 0.0)

    qkv = turn(by_block(qkv, tok), (cos_q, cos_kv), (sin_q, sin_kv)).astype(bf16)
    q = qkv[:, :HEAD]
    own_kv = by_core(qkv[:, HEAD:])
    kv_parts = []
    for k in range(count_b):
        here = rotated(own_kv, "b", k) if k else own_kv
        if k == 1:
            here, gate_mine, up_pack = join(here, gate_mine, up_pack)
            up_mine = exchange(up_pack)
        for j in range(count_y):
            kv_parts.append(rotated(here, "y", j) if j else here)
    kv_mine = jnp.concatenate(kv_parts, axis=0)
    kv_mine, gate_mine, up_mine, down_pack = join(kv_mine, gate_mine, up_mine, down_pack)
    gate_w = gather_rows(gate_mine)
    kv = jnp.stack([kv_mine, swapped(kv_mine, "c")])
    down_mine = exchange(down_pack)
    up_w = gather_rows(up_mine)
    keys = kv.shape[1]
    attended, lse = attention_forward(
        q, kv, meta_forward, q_pos[:, None], k_pos.reshape(-1, 1, BLOCK), q_block
    )
    attended, down_mine = join(attended, down_mine)
    down_w = gather_rows(down_mine)
    attended_b = by_block(attended.astype(bf16), tok)
    size = 2 * tok

    def cut(values):
        return [values[i * size : (i + 1) * size] for i in range(RING)]

    projected, _ = scatter_tokens([dot_nt(part, out_w).astype(bf16) for part in cut(attended_b)])
    r2 = lax.rsqrt(mean(projected * projected) + EPS)
    hidden = x + projected * r2 * g_attn_out

    r3 = lax.rsqrt(mean(hidden * hidden) + EPS)
    def mlp_forward(i, part):
        gate = dot_nn(part, gate_w).astype(bf16)
        up = dot_nn(part, up_w).astype(bf16)
        return gate, up, (gelu_parts(gate.astype(f32))[0] * up.astype(f32)).astype(bf16)

    x2, mlp, _ = gather_tokens((hidden * r3).astype(bf16), mlp_forward)
    gate, up, mixed = zip(*mlp)
    reduced, _ = scatter_tokens([dot_nt(part, down_w).astype(bf16) for part in mixed])
    r4 = lax.rsqrt(mean(reduced * reduced) + EPS)

    top = copies_first(cotangent).astype(f32)
    lifted = top * g_mlp_out
    d_reduced = r4 * lifted - reduced * (r4 * r4 * r4 * mean(lifted * reduced))
    def mlp_backward(i, part):
        d_mixed = dot_nn(part, down_w)
        gelu, slope = gelu_parts(gate[i].astype(f32))
        d_gate = (d_mixed * up[i].astype(f32) * slope).astype(bf16)
        d_up = (d_mixed * gelu).astype(bf16)
        return d_gate, d_up, (dot_nt(d_gate, gate_w) + dot_nt(d_up, up_w)).astype(bf16)

    x3, mlp, _ = gather_tokens(d_reduced.astype(bf16), mlp_backward)
    d_gate, d_up, dn3 = zip(*mlp)
    x2 = jnp.concatenate(x2, axis=0)
    x3 = jnp.concatenate(x3, axis=0)
    down_part = dot_tn(x3, jnp.concatenate(mixed, axis=0)).astype(bf16)
    gate_part = dot_tn(x2, jnp.concatenate(d_gate, axis=0)).astype(bf16)
    up_part = dot_tn(x2, jnp.concatenate(d_up, axis=0)).astype(bf16)
    dn3, parts = scatter_tokens(dn3, ((down_part,), (gate_part,), (up_part,)))
    down_rows, gate_rows, up_rows = [scatter_rows(part[0]) for part in parts]
    d_hidden = top + r3 * dn3 - hidden * (r3 * r3 * r3 * mean(dn3 * hidden))
    lifted = d_hidden * g_attn_out
    d_projected = r2 * lifted - projected * (r2 * r2 * r2 * mean(lifted * projected))
    d_projected, d_hidden, reduced = join(d_projected.astype(bf16), d_hidden, reduced)
    output = copies_back((hidden + reduced * r4 * g_mlp_out).astype(bf16))
    d_gain_mlp_out = jnp.sum(top * reduced * r4, axis=0, keepdims=True)
    d_gain_attn_out = jnp.sum(d_hidden * projected * r2, axis=0, keepdims=True)
    d_gains = jnp.concatenate(
        [
            moved(d_gain_attn_out, count_b * count_y, RING).reshape(-1, rows),
            moved(d_gain_mlp_out, count_b * count_y, RING).reshape(-1, rows),
        ],
        axis=1,
    )
    d_gains = scatter_small(d_gains)
    x4, d_attended, ((output,), _, _) = gather_tokens(
        d_projected, lambda i, part: (dot_nn(part, out_w).astype(bf16),), ((output,), None, None)
    )
    d_attended = by_block(jnp.concatenate([part[0] for part in d_attended], axis=0), tok)
    out_part = dot_tn(jnp.concatenate(x4, axis=0), attended_b).astype(bf16)
    delta = jnp.sum(d_attended.astype(f32) * attended, axis=1)
    delta, down_rows, out_part, d_gains = join(delta, down_rows, out_part, d_gains)
    out_rows = scatter_rows(out_part)
    down_sum = exchange(down_rows)
    d_query, d_kv = attention_backward(
        q,
        d_attended,
        kv,
        meta_backward,
        lse.reshape(1, -1),
        delta[None],
        q_pos[None],
        k_pos[:, None],
    )
    d_query, d_kv, down_sum, gate_rows, up_rows = join(
        d_query, d_kv, down_sum, gate_rows, up_rows
    )
    gate_sum = exchange(gate_rows)
    d_mine = (d_kv[0].astype(f32) + swapped(d_kv[1], "c").astype(f32)).astype(bf16)
    d_parts = d_mine.reshape(count_b, count_y, keys // (count_b * count_y), HEAD)
    d_own = None
    for k in list(range(1, count_b)) + [0]:
        piece = d_parts[k, 0].astype(f32)
        for j in range(1, count_y):
            piece = piece + rotated(d_parts[k, j], "y", -j).astype(f32)
        if k == 1:
            piece, gate_sum, up_rows = join(piece, gate_sum, up_rows)
            up_sum = exchange(up_rows)
        if k:
            piece = rotated(piece.astype(bf16), "b", -k).astype(f32)
        d_own = piece if d_own is None else d_own + piece
    d_own, up_sum, out_rows = join(d_own, up_sum, out_rows)
    out_sum = exchange(out_rows)
    d_q = turn(d_query, (cos_q,), (-sin_q,)).astype(bf16)
    d_k = turn(by_core(d_own), (cos_kv,), (-sin_kv,)).astype(bf16)
    d_qkv = by_block(jnp.concatenate([d_q, d_k], axis=1), tok)
    qkv_part = dot_tn(jnp.concatenate(x1, axis=0), d_qkv).astype(bf16)
    d_qkv, qkv_part = join(d_qkv, qkv_part)
    qkv_rows = scatter_rows(qkv_part)
    dn1, ((out_sum,), _, _) = scatter_tokens(
        [dot_nt(part, qkv_w).astype(bf16) for part in cut(d_qkv)], ((out_sum,), None, None)
    )
    qkv_sum = exchange(qkv_rows)
    down_sum, gate_sum, up_sum, out_sum, qkv_sum = [
        part.astype(f32) for part in (down_sum, gate_sum, up_sum, out_sum, qkv_sum)
    ]
    d_source = r1 * dn1 - x * (r1 * r1 * r1 * mean(dn1 * x))
    input_grad = copies_back((d_hidden + d_source).astype(bf16))

    q_sum = join_cols(qkv_sum[:, :, :HEAD])
    kv_sum = qkv_sum[:, :, HEAD:].reshape(KV_HEADS, 2, rows, HEAD)
    k_sum, v_sum = join_cols(kv_sum[:, 0]), join_cols(kv_sum[:, 1])
    gate_sum, up_sum = join_cols(gate_sum), join_cols(up_sum)

    def row_term(weight, grad):
        return jnp.sum(weight.astype(f32) * grad, axis=1)

    d_gain_attn_in = (
        row_term(w_query, q_sum) + row_term(w_key, k_sum) + row_term(w_value, v_sum)
    )
    d_gain_mlp_in = row_term(w_gate, gate_sum) + row_term(w_up, up_sum)
    return (
        output,
        input_grad,
        q_sum * g_attn,
        k_sum * g_attn,
        v_sum * g_attn,
        join_cols(out_sum),
        gate_sum * g_mlp,
        up_sum * g_mlp,
        join_cols(down_sum),
        d_gain_attn_in,
        d_gains[:rows],
        d_gain_mlp_in,
        d_gains[rows:],
    )


def solution(mesh):
    ctx, fsdp = mesh.devices.shape
    laid = Mesh(mesh.devices.reshape(RING, ctx // RING, fsdp // 2, 2), AXES)
    rows = P(AXES, None)
    line = P(AXES)
    return jax.shard_map(
        body,
        mesh=laid,
        in_specs=(rows,) * 9 + (line,) * 4,
        out_specs=(rows,) * 9 + (line,) * 4,
        check_vma=False,
    )
```

```python
import jax
import jax.numpy as jnp
from jax import lax
from jax.experimental import pallas as pl
from jax.experimental.pallas import tpu as pltpu
from jax.sharding import Mesh
from jax.sharding import PartitionSpec as P

HEADS = 8
KV_HEADS = 4
HEAD = 256
WINDOW = 4096
CAP = 10.0
EPS = 1e-06
SCALE = HEAD**-0.5
BLOCK = 256

RING = 4
AXES = ("z", "b", "y", "c")
GROUP = ("z", "c")
COPIES = ("b", "y")

bf16 = jnp.bfloat16
f32 = jnp.float32


def swapped(value, axis):
    return lax.ppermute(value, axis, [(0, 1), (1, 0)])


def rotated(value, axis, steps):
    count = lax.axis_size(axis)
    return lax.ppermute(value, axis, [(i, (i + steps) % count) for i in range(count)])


def copies_apart():
    return [(k, j) for k in range(lax.axis_size("b")) for j in range(lax.axis_size("y"))]


def moved_on(value, k, j, back=False):
    if k == 0 and j == 0:
        return value
    count_b, count_y = lax.axis_size("b"), lax.axis_size("y")
    pairs = [
        (b * count_y + y, (b + k) % count_b * count_y + (y + j) % count_y)
        for b in range(count_b)
        for y in range(count_y)
    ]
    return lax.ppermute(value, COPIES, [(t, f) if back else (f, t) for f, t in pairs])


def join(*values):
    return lax.optimization_barrier(values)


def dot_nn(left, right):
    return lax.dot_general(left, right, (((1,), (0,)), ((), ())), preferred_element_type=f32)


def dot_nt(left, right):
    return lax.dot_general(left, right, (((1,), (1,)), ((), ())), preferred_element_type=f32)


def dot_tn(left, right):
    return lax.dot_general(left, right, (((0,), (0,)), ((), ())), preferred_element_type=f32)


def moved(values, first, second):
    rest = values.shape[1] // (first * second)
    starts = [(i * second + j) * rest for j in range(second) for i in range(first)]
    return jnp.concatenate([values[:, s : s + rest] for s in starts], axis=1)


def copies_first(values, normed=False):
    rows, width = values.shape
    copies = lax.axis_size("b") * lax.axis_size("y")

    def kernel(in_ref, out_ref, *normed_refs):
        here = moved(in_ref[...].astype(f32), RING, copies)
        out_ref[...] = here.astype(out_ref.dtype)
        if normed:
            inverse = lax.rsqrt(jnp.mean(here * here, axis=1, keepdims=True) + EPS)
            normed_refs[0][...] = (here * inverse).astype(bf16)
            normed_refs[1][...] = inverse

    out_shape = [jax.ShapeDtypeStruct((rows, width), values.dtype)]
    if normed:
        out_shape.append(jax.ShapeDtypeStruct((rows, width), bf16))
        out_shape.append(jax.ShapeDtypeStruct((rows, 1), f32))
    result = pl.pallas_call(
        kernel,
        out_shape=out_shape,
        compiler_params=pltpu.CompilerParams(vmem_limit_bytes=24 << 20),
        cost_estimate=pl.CostEstimate(
            flops=rows * width, bytes_accessed=8 * rows * width, transcendentals=0
        ),
        name="copies_first",
    )(values)
    return result if normed else result[0]


def copies_back(values):
    rows, width = values.shape
    copies = lax.axis_size("b") * lax.axis_size("y")

    def kernel(in_ref, out_ref):
        out_ref[...] = moved(in_ref[...].astype(f32), copies, RING).astype(out_ref.dtype)

    return pl.pallas_call(
        kernel,
        out_shape=jax.ShapeDtypeStruct((rows, width), values.dtype),
        compiler_params=pltpu.CompilerParams(vmem_limit_bytes=24 << 20),
        cost_estimate=pl.CostEstimate(
            flops=rows * width, bytes_accessed=8 * rows * width, transcendentals=0
        ),
        name="copies_back",
    )(values)


def round_ring(value):
    pairs = [(2 * i, (i + 1) % RING * 2) for i in range(RING)]
    pairs += [(2 * i + 1, (i - 1) % RING * 2 + 1) for i in range(RING)]
    return lax.ppermute(value, GROUP, pairs)


def gather_tokens(own, work=None, beside=(None, None, None)):
    here = own
    chunks, results = [jnp.concatenate([own, swapped(own, "c")], axis=0)], []
    beside = list(beside)
    for step in range(RING):
        results.append(work(step, chunks[step]) if work else ())
        if step == RING - 1:
            return chunks, results, beside
        here = round_ring(here)
        extra = beside[step] or ()
        if results[step] or extra:
            here, results[step], beside[step] = join(here, results[step], extra)
        chunks.append(jnp.concatenate([here, swapped(here, "c")], axis=0))


def relative_places():
    place = None
    for axis in AXES:
        count = lax.axis_size(axis)
        at = (lax.axis_index(axis) - jnp.arange(count, dtype=jnp.int32)) % count
        place = at if place is None else (place[:, None] * count + at[None, :]).reshape(-1)
    return place


def gather_small(value):
    for axis in AXES[::-1]:
        parts = [value] + [rotated(value, axis, k) for k in range(1, lax.axis_size(axis))]
        value = jnp.concatenate(parts, axis=0)
    place = relative_places()
    chosen = place[None, :] == jnp.arange(place.shape[0], dtype=jnp.int32)[:, None]
    return dot_nn(chosen.astype(value.dtype), value)


def scatter_small(value):
    place = relative_places()
    chosen = place[:, None] == jnp.arange(place.shape[0], dtype=jnp.int32)[None, :]
    value = jnp.dot(
        chosen.astype(f32), value, precision=lax.Precision.HIGHEST, preferred_element_type=f32
    )
    for axis in AXES:
        count = lax.axis_size(axis)
        parts = value.reshape(count, -1, value.shape[1])
        total = parts[0]
        for k in range(1, count):
            total = total + rotated(parts[k], axis, -k)
        value = total
    return value[0]


def scatter_tokens(chunks, beside=(None, None, None)):
    rows = chunks[0].shape[0] // 2
    carried = None
    beside = list(beside)
    for step in range(RING):
        chunk = chunks[(step + 1) % RING]
        here = chunk[:rows].astype(f32) + swapped(chunk[rows:], "c").astype(f32)
        if carried is not None:
            here = here + carried.astype(f32)
        if step == RING - 1:
            return here, beside
        carried = round_ring(here.astype(bf16))
        if callable(beside[step]):
            beside[step] = beside[step](beside[step - 1])
        if beside[step] is not None:
            carried, *beside[step] = join(carried, *beside[step])


def exchange(blocks):
    return lax.all_to_all(blocks, GROUP, split_axis=0, concat_axis=0, tiled=True)


def gather_rows(blocks):
    parts, rows, cols = blocks.shape
    return lax.all_gather(blocks.reshape(parts * rows, cols), COPIES, axis=0, tiled=True)


def scatter_rows(grad):
    total = lax.psum_scatter(grad, COPIES, scatter_dimension=0, tiled=True)
    return total.reshape(8, -1, grad.shape[1])


def split_cols(weight):
    rows, cols = weight.shape
    return weight.reshape(rows, 8, cols // 8).transpose(1, 0, 2)


def join_cols(blocks):
    parts, rows, cols = blocks.shape
    return blocks.transpose(1, 0, 2).reshape(rows, parts * cols)


def attention_forward(q, kv_mine, kv_other, meta, run):
    tokens = q.shape[0]
    keys = kv_mine.shape[0]
    block = 2 * run
    q_runs = tokens // run
    steps = tokens // block

    def kernel(meta_ref, q_ref, mine_ref, other_ref, o_ref, lse_ref, acc_ref, sum_ref):
        i = pl.program_id(0)
        core = meta_ref[0]
        q_lows = [meta_ref[1 + 2 * i], meta_ref[2 + 2 * i]]
        acc_ref[...] = jnp.zeros_like(acc_ref)
        sum_ref[...] = jnp.zeros_like(sum_ref)
        lane = lax.broadcasted_iota(jnp.int32, (1, block), 1)
        row = lax.broadcasted_iota(jnp.int32, (block, 1), 0)
        q_pos = row + jnp.where(row < run, q_lows[0], q_lows[1] - run)

        def step(j, carry):
            one = meta_ref[1 + q_runs + 2 * j]
            two = meta_ref[2 + q_runs + 2 * j]

            used = [
                (q_low + run > low) & (q_low - (low + run) < WINDOW)
                for q_low in q_lows
                for low in (one, two)
            ]

            @pl.when(used[0] | used[1] | used[2] | used[3])
            def _():
                place = pl.ds(pl.multiple_of(j * block, block), block)
                mine, other = mine_ref[place, :], other_ref[place, :]
                key = jnp.where(core == 0, mine, other)
                value = jnp.where(core == 0, other, mine)
                scores = dot_nt(q_ref[...], key)
                turned = jnp.tanh(scores * (SCALE / CAP))
                k_pos = lane + jnp.where(lane < run, one, two - run)
                away = q_pos - k_pos
                weight = jnp.where((away >= 0) & (away < WINDOW), jnp.exp(turned * CAP), 0.0)
                sum_ref[...] += jnp.sum(weight, axis=1, keepdims=True)
                acc_ref[...] += dot_nn(weight.astype(bf16), value)

            return carry

        lax.fori_loop(0, keys // block, step, 0)
        total = sum_ref[...]
        o_ref[...] = acc_ref[...] / total
        lse_ref[...] = jnp.log(total)

    return pl.pallas_call(
        kernel,
        grid=(steps,),
        in_specs=[
            pl.BlockSpec(memory_space=pltpu.SMEM),
            pl.BlockSpec((block, HEAD), lambda i: (i, 0)),
            pl.BlockSpec(memory_space=pltpu.VMEM),
            pl.BlockSpec(memory_space=pltpu.VMEM),
        ],
        out_specs=[
            pl.BlockSpec((block, HEAD), lambda i: (i, 0)),
            pl.BlockSpec((block, 1), lambda i: (i, 0)),
        ],
        out_shape=[
            jax.ShapeDtypeStruct((tokens, HEAD), f32),
            jax.ShapeDtypeStruct((tokens, 1), f32),
        ],
        scratch_shapes=[pltpu.VMEM((block, HEAD), f32), pltpu.VMEM((block, 1), f32)],
        compiler_params=pltpu.CompilerParams(vmem_limit_bytes=4 * kv_mine.size + (12 << 20)),
        cost_estimate=pl.CostEstimate(
            flops=4 * tokens * keys * HEAD,
            bytes_accessed=4 * kv_mine.size + 8 * tokens * HEAD,
            transcendentals=2 * tokens * keys,
        ),
        name="attention_forward",
    )(meta, q, kv_mine, kv_other)


def attention_backward(q, d_out, kv_mine, kv_other, meta, lse, delta, run):
    tokens = q.shape[0]
    keys = kv_mine.shape[0]
    q_block = 2 * run
    block_k = 2 * run
    steps = tokens // q_block
    key_steps = keys // block_k
    q_runs, last = tokens // run, keys // run - 1

    def kernel(
        meta_ref, q_ref, d_ref, mine_ref, other_ref, lse_ref, delta_ref,
        dq_ref, d_mine_ref, d_other_ref, key_acc, value_acc, key_ref, value_ref,
    ):
        j = pl.program_id(0)
        core = meta_ref[0]
        at = j * block_k
        one = at // run
        two = jnp.minimum((at + block_k - 1) // run, last)
        one_pos = meta_ref[1 + q_runs + one] + at - one * run
        two_pos = meta_ref[1 + q_runs + two] + at - two * run
        turn_at = jnp.minimum((one + 1) * run - at, block_k)
        row = lax.broadcasted_iota(jnp.int32, (block_k, 1), 0)
        k_pos = row + jnp.where(row < turn_at, one_pos, two_pos)
        k_runs = [(one_pos, turn_at), (two_pos + turn_at, block_k - turn_at)]

        @pl.when(j == 0)
        def _():
            dq_ref[...] = jnp.zeros_like(dq_ref)

        key_acc[...] = jnp.zeros_like(key_acc)
        value_acc[...] = jnp.zeros_like(value_acc)
        key_ref[...] = jnp.where(core == 0, mine_ref[...], other_ref[...])
        value_ref[...] = jnp.where(core == 0, other_ref[...], mine_ref[...])
        for i in range(steps):
            q_runs_here = []
            first = i * q_block
            while first < (i + 1) * q_block:
                number = first // run
                stop = min((number + 1) * run, (i + 1) * q_block)
                q_runs_here.append((first, stop, meta_ref[1 + number] - number * run))
                first = stop
            used = None
            for first, stop, q_shift in q_runs_here:
                for low, size in k_runs:
                    here = (q_shift + stop > low) & (q_shift + first - (low + size) < WINDOW)
                    here = here & (size > 0)
                    used = here if used is None else used | here

            @pl.when(used)
            def _(i=i, q_runs_here=q_runs_here):
                place = pl.ds(i * q_block, q_block)
                key = key_ref[...]
                value = value_ref[...]
                query = q_ref[place, :]
                d_here = d_ref[place, :]
                turned = jnp.tanh(dot_nt(key, query) * (SCALE / CAP))
                lane = lax.broadcasted_iota(jnp.int32, (1, q_block), 1) + i * q_block
                q_pos = lane + q_runs_here[-1][2]
                for first, stop, q_shift in q_runs_here[-2::-1]:
                    q_pos = jnp.where(lane < stop, lane + q_shift, q_pos)
                away = q_pos - k_pos
                soft = jnp.where(
                    (away >= 0) & (away < WINDOW),
                    jnp.exp(turned * CAP - lse_ref[:, place]),
                    0.0,
                )
                d_prob = dot_nt(value, d_here)
                d_raw = soft * (d_prob - delta_ref[:, place]) * (1.0 - turned * turned)
                d_raw = d_raw.astype(bf16)
                value_acc[...] += dot_nn(soft.astype(bf16), d_here)
                key_acc[...] += dot_nn(d_raw, query)
                dq_ref[place, :] += dot_tn(d_raw, key)

        d_key, d_value = (key_acc[...] * SCALE).astype(bf16), value_acc[...].astype(bf16)
        d_mine_ref[...] = jnp.where(core == 0, d_key, d_value)
        d_other_ref[...] = jnp.where(core == 0, d_value, d_key)

        @pl.when(j == key_steps - 1)
        def _():
            dq_ref[...] = dq_ref[...] * SCALE

    whole = pl.BlockSpec(memory_space=pltpu.VMEM)
    block = pl.BlockSpec((block_k, HEAD), lambda j: (j, 0))
    return pl.pallas_call(
        kernel,
        grid=(key_steps,),
        in_specs=[
            pl.BlockSpec(memory_space=pltpu.SMEM),
            whole,
            whole,
            block,
            block,
            whole,
            whole,
        ],
        out_specs=[whole, block, block],
        out_shape=[
            jax.ShapeDtypeStruct((tokens, HEAD), f32),
            jax.ShapeDtypeStruct((keys, HEAD), bf16),
            jax.ShapeDtypeStruct((keys, HEAD), bf16),
        ],
        scratch_shapes=[
            pltpu.VMEM((block_k, HEAD), f32),
            pltpu.VMEM((block_k, HEAD), f32),
            pltpu.VMEM((block_k, HEAD), bf16),
            pltpu.VMEM((block_k, HEAD), bf16),
        ],
        compiler_params=pltpu.CompilerParams(vmem_limit_bytes=24 << 20),
        cost_estimate=pl.CostEstimate(
            flops=10 * tokens * keys * HEAD,
            bytes_accessed=8 * kv_mine.size + 8 * tokens * HEAD,
            transcendentals=2 * tokens * keys,
        ),
        name="attention_backward",
    )(meta, q, d_out, kv_mine, kv_other, lse, delta)


def rotated_halves(values, cosine, sine):
    half = HEAD // 2
    a, b = values[:, :half], values[:, half:]
    return jnp.concatenate([a * cosine - b * sine, b * cosine + a * sine], axis=1)


BACK = [0] + list(range(RING - 1, 0, -1))


def call_on_rows(kernel, name, out_shape, *operands):
    size = sum(x.size * x.dtype.itemsize for x in operands)
    return pl.pallas_call(
        kernel,
        in_specs=[pl.BlockSpec(memory_space=pltpu.SMEM)]
        + [pl.BlockSpec(memory_space=pltpu.VMEM)] * (len(operands) - 1),
        out_shape=out_shape,
        compiler_params=pltpu.CompilerParams(vmem_limit_bytes=24 << 20),
        cost_estimate=pl.CostEstimate(flops=size, bytes_accessed=2 * size, transcendentals=0),
        name=name,
    )(*operands)


def to_blocks(chunks, core, tables=None):
    tok, width = chunks[0].shape[0] // 2, chunks[0].shape[1]
    heads = width // HEAD

    def kernel(core_ref, *refs):
        first = core_ref[0] == 0
        outs = refs[-heads:]
        for d in range(RING):
            for e in range(2):
                one = refs[BACK[d] if e else d][e * tok : (e + 1) * tok, :]
                two = refs[BACK[d] if e else d][(1 - e) * tok : (2 - e) * tok, :]
                here = jnp.where(first, one, two)
                place = pl.ds((2 * d + e) * tok, tok)
                for h in range(heads):
                    part = here[:, h * HEAD : (h + 1) * HEAD]
                    if tables is not None:
                        cosine, sine = refs[RING][place, :], refs[RING + 1][place, :]
                        turned = rotated_halves(part, cosine, sine)
                        part = jnp.where(first, turned, part) if h else turned
                    outs[h][place, :] = part.astype(bf16)

    shape = jax.ShapeDtypeStruct((2 * RING * tok, HEAD), bf16)
    return call_on_rows(kernel, "to_blocks", [shape] * heads, core, *chunks, *(tables or ()))


def to_chunks(values, core, tables=None, keyed=False):
    tok = values.shape[0] // (2 * RING)

    def kernel(core_ref, *refs):
        first = core_ref[0] == 0
        for s in range(RING):
            for p in range(2):
                parts = []
                for d, e in ((BACK[s] if p else s, p), (s if p else BACK[s], 1 - p)):
                    place = pl.ds((2 * d + e) * tok, tok)
                    part = refs[0][place, :]
                    if tables is not None:
                        cosine, sine = refs[1][place, :], refs[2][place, :]
                        turned = rotated_halves(part, cosine, -sine)
                        part = jnp.where(first, turned, part) if keyed else turned
                    parts.append(part)
                here = jnp.where(first, parts[0], parts[1])
                refs[-1][pl.ds((2 * s + p) * tok, tok), :] = here.astype(bf16)

    shape = jax.ShapeDtypeStruct(values.shape, bf16)
    return call_on_rows(kernel, "to_chunks", shape, core, values, *(tables or ()))


def mean(values):
    return jnp.mean(values, axis=1, keepdims=True)


def gelu_parts(u):
    k = 0.7978845608028654
    t = jnp.tanh(k * (u + 0.044715 * u * u * u))
    value = 0.5 * u * (1.0 + t)
    slope = 0.5 * (1.0 + t) + 0.5 * u * (1.0 - t * t) * k * (1.0 + 3 * 0.044715 * u * u)
    return value, slope


def body(
    inputs,
    cotangent,
    w_query,
    w_key,
    w_value,
    w_out_t,
    w_gate,
    w_up,
    w_down_t,
    gain_attn_in,
    gain_attn_out,
    gain_mlp_in,
    gain_mlp_out,
):
    tok, width = inputs.shape
    rows = w_query.shape[0]
    count_b, count_y = lax.axis_size("b"), lax.axis_size("y")
    z, b, y, c = [lax.axis_index(name) for name in AXES]

    g_attn = gain_attn_in.astype(f32)[:, None]
    g_mlp = gain_mlp_in.astype(f32)[:, None]

    def scaled(weight, gain):
        return (weight.astype(f32) * gain).astype(bf16)

    pairs = jnp.stack(
        [w_key.reshape(rows, KV_HEADS, HEAD), w_value.reshape(rows, KV_HEADS, HEAD)], axis=2
    ).reshape(rows, 8, HEAD)
    qkv_pack = jnp.concatenate([w_query.reshape(rows, 8, HEAD), pairs], axis=2)
    qkv_pack = (qkv_pack.astype(f32) * g_attn[:, :, None]).astype(bf16)
    qkv_pack = jnp.concatenate([qkv_pack, w_out_t.reshape(rows, 8, HEAD)], axis=2)
    qkv_pack = qkv_pack.transpose(1, 0, 2)
    x, normed_x, r1 = copies_first(inputs, normed=True)
    x = x.astype(f32)
    gate_pack = split_cols(scaled(w_gate, g_mlp))
    up_pack = split_cols(scaled(w_up, g_mlp))
    down_pack = split_cols(w_down_t)
    qkv_w = gather_rows(exchange(qkv_pack))
    qkv_w, out_w = qkv_w[:, : 2 * HEAD], qkv_w[:, 2 * HEAD :]
    gains = jnp.concatenate([gain_attn_out, gain_mlp_out])[None]
    gains = gather_small(gains)
    x1, _, (_, _, (gate_pack,)) = gather_tokens(normed_x, None, (None, None, (gate_pack,)))
    gate_mine = exchange(gate_pack)
    qkv = [dot_nn(part, qkv_w) for part in x1]
    run = 2 * tok

    def starts(places_b, places_y):
        blocks = (z - jnp.arange(RING, dtype=jnp.int32)) % RING
        place = (blocks * count_b + places_b[:, None, None]) * count_y + places_y[:, None]
        return place.reshape(-1) * run

    q_starts = starts(b[None], y[None])
    k_starts = starts(
        (b - jnp.arange(count_b, dtype=jnp.int32)) % count_b,
        (y - jnp.arange(count_y, dtype=jnp.int32)) % count_y,
    )
    meta = jnp.concatenate([c.astype(jnp.int32)[None], q_starts, k_starts])

    core = c.astype(jnp.int32)[None]
    q_pos = (q_starts[:, None] + jnp.arange(run, dtype=jnp.int32)).reshape(-1)
    frequency = 10000.0 ** (-jnp.arange(HEAD // 2, dtype=f32) * 2.0 / HEAD)
    angles = q_pos.astype(f32)[:, None] * frequency[None, :]
    tables = (jnp.cos(angles), jnp.sin(angles))

    q, own_kv = to_blocks(qkv, core, tables)
    kv_mine = jnp.concatenate([moved_on(own_kv, k, j) for k, j in copies_apart()], axis=0)
    kv_mine, gate_mine, up_pack, gains = join(kv_mine, gate_mine, up_pack, gains)
    ff_cols = w_gate.shape[1] // 8
    gate_w = gather_rows(gate_mine)
    up_mine = exchange(up_pack)
    kv_other = swapped(kv_mine, "c")
    attended, lse = attention_forward(q, kv_mine, kv_other, meta, run)
    attended, up_mine, down_pack = join(attended, up_mine, down_pack)
    up_w = gather_rows(up_mine)
    down_mine = exchange(down_pack)
    g_attn_out = moved(gains[:, :rows].reshape(1, width), RING, count_b * count_y)
    g_mlp_out = moved(gains[:, rows:].reshape(1, width), RING, count_b * count_y)
    attended_b = to_chunks(attended, core)
    size = 2 * tok

    def cut(values):
        return [values[i * size : (i + 1) * size] for i in range(RING)]

    projected, ((gate_w,), (down_mine,), _) = scatter_tokens(
        [dot_nt(part, out_w).astype(bf16) for part in cut(attended_b)],
        ((gate_w,), (down_mine,), None),
    )
    down_w = gather_rows(down_mine)
    r2 = lax.rsqrt(mean(projected * projected) + EPS)
    hidden = x + projected * r2 * g_attn_out

    r3 = lax.rsqrt(mean(hidden * hidden) + EPS)
    def mlp_forward(i, part):
        gate = dot_nn(part, gate_w).astype(bf16)
        up = dot_nn(part, up_w).astype(bf16)
        return gate, up, (gelu_parts(gate.astype(f32))[0] * up.astype(f32)).astype(bf16)

    x2, mlp, _ = gather_tokens((hidden * r3).astype(bf16), mlp_forward)
    gate, up, mixed = zip(*mlp)
    *x1, hidden = join(*x1, hidden)
    x1, x2, all_mixed = [jnp.concatenate(parts, axis=0) for parts in (x1, x2, mixed)]
    reduced, ((x2,), (x1, all_mixed), _) = scatter_tokens(
        [dot_nt(part, down_w).astype(bf16) for part in mixed], ((x2,), (x1, all_mixed), None)
    )
    r4 = lax.rsqrt(mean(reduced * reduced) + EPS)

    top = copies_first(cotangent).astype(f32)
    lifted = top * g_mlp_out
    d_reduced = r4 * lifted - reduced * (r4 * r4 * r4 * mean(lifted * reduced))
    def mlp_backward(i, part):
        d_mixed = dot_nn(part, down_w)
        gelu, slope = gelu_parts(gate[i].astype(f32))
        d_gate = (d_mixed * up[i].astype(f32) * slope).astype(bf16)
        d_up = (d_mixed * gelu).astype(bf16)
        return d_gate, d_up, (dot_nt(d_gate, gate_w) + dot_nt(d_up, up_w)).astype(bf16)

    x3, mlp, _ = gather_tokens(d_reduced.astype(bf16), mlp_backward)
    d_gate, d_up, dn3 = zip(*mlp)
    x3 = jnp.concatenate(x3, axis=0)
    down_part = dot_tn(x3, all_mixed).astype(bf16)
    gate_part = dot_tn(x2, jnp.concatenate(d_gate, axis=0)).astype(bf16)
    up_part = dot_tn(x2, jnp.concatenate(d_up, axis=0)).astype(bf16)
    dn3, ((down_part,), (gate_part,), (up_part,)) = scatter_tokens(
        dn3, ((down_part,), (gate_part,), (up_part,))
    )
    down_rows, gate_rows, up_rows = [scatter_rows(p) for p in (down_part, gate_part, up_part)]
    d_hidden = top + r3 * dn3 - hidden * (r3 * r3 * r3 * mean(dn3 * hidden))
    lifted = d_hidden * g_attn_out
    d_projected = r2 * lifted - projected * (r2 * r2 * r2 * mean(lifted * projected))
    d_projected, d_hidden, reduced = join(d_projected.astype(bf16), d_hidden, reduced)
    output = copies_back((hidden + reduced * r4 * g_mlp_out).astype(bf16))
    d_gain_mlp_out = jnp.sum(top * reduced * r4, axis=0, keepdims=True)
    d_gain_attn_out = jnp.sum(d_hidden * projected * r2, axis=0, keepdims=True)
    d_gains = jnp.concatenate(
        [
            moved(d_gain_attn_out, count_b * count_y, RING).reshape(-1, rows),
            moved(d_gain_mlp_out, count_b * count_y, RING).reshape(-1, rows),
        ],
        axis=1,
    )
    d_gains = scatter_small(d_gains)
    x4, d_attended, ((output,), _, _) = gather_tokens(
        d_projected, lambda i, part: (dot_nn(part, out_w).astype(bf16),), ((output,), None, None)
    )
    (d_attended,) = to_blocks([part[0] for part in d_attended], core)
    delta = jnp.sum(d_attended.astype(f32) * attended, axis=1)
    delta, down_rows, gate_rows, d_gains = join(delta, down_rows, gate_rows, d_gains)
    down_sum = exchange(down_rows)
    d_query, d_mine, d_other = attention_backward(
        q, d_attended, kv_mine, kv_other, meta, lse.reshape(1, -1), delta[None], run
    )
    d_query, d_mine, d_other, down_sum, gate_rows = join(
        d_query, d_mine, d_other, down_sum, gate_rows
    )
    gate_sum = exchange(gate_rows)
    d_mine = (d_mine.astype(f32) + swapped(d_other, "c").astype(f32)).astype(bf16)
    d_parts = d_mine.reshape(count_b * count_y, -1, HEAD)
    d_own = sum(
        moved_on(part, k, j, back=True).astype(f32) for part, (k, j) in zip(d_parts, copies_apart())
    )
    d_own, d_query, *x4, gate_sum, up_rows = join(d_own, d_query, *x4, gate_sum, up_rows)
    up_sum = exchange(up_rows)
    d_q = to_chunks(d_query, core, tables)
    d_k = to_chunks(d_own, core, tables, keyed=True)
    d_qkv = jnp.concatenate([d_q, d_k], axis=1)
    q_part = dot_tn(x1, d_q)
    out_part = dot_tn(jnp.concatenate(x4, axis=0), attended_b)
    q_part = jnp.concatenate([q_part, out_part], axis=1).astype(bf16)
    kv_part = dot_tn(x1, d_k).astype(bf16)
    d_qkv, q_part, kv_part = join(d_qkv, q_part, kv_part)
    q_rows, kv_rows = scatter_rows(q_part), scatter_rows(kv_part)
    dn1, (_, (up_sum, _), (q_sum, kv_rows)) = scatter_tokens(
        [dot_nt(part, qkv_w).astype(bf16) for part in cut(d_qkv)],
        (None, (up_sum, q_rows), lambda before: (exchange(before[1]), kv_rows)),
    )
    kv_sum = exchange(kv_rows)
    down_sum, gate_sum, up_sum, q_sum, kv_sum = [
        part.astype(f32) for part in (down_sum, gate_sum, up_sum, q_sum, kv_sum)
    ]
    q_sum, out_sum = join_cols(q_sum[:, :, :HEAD]), join_cols(q_sum[:, :, HEAD:])
    kv_sum = kv_sum.reshape(KV_HEADS, 2, rows, HEAD)
    d_source = r1 * dn1 - x * (r1 * r1 * r1 * mean(dn1 * x))
    input_grad = copies_back((d_hidden + d_source).astype(bf16))

    k_sum, v_sum = join_cols(kv_sum[:, 0]), join_cols(kv_sum[:, 1])
    gate_sum, up_sum = join_cols(gate_sum), join_cols(up_sum)

    def row_term(weight, grad):
        return jnp.sum(weight.astype(f32) * grad, axis=1)

    d_gain_attn_in = (
        row_term(w_query, q_sum) + row_term(w_key, k_sum) + row_term(w_value, v_sum)
    )
    d_gain_mlp_in = row_term(w_gate, gate_sum) + row_term(w_up, up_sum)
    return (
        output,
        input_grad,
        q_sum * g_attn,
        k_sum * g_attn,
        v_sum * g_attn,
        out_sum,
        gate_sum * g_mlp,
        up_sum * g_mlp,
        join_cols(down_sum),
        d_gain_attn_in,
        d_gains[:rows],
        d_gain_mlp_in,
        d_gains[rows:],
    )


def solution(mesh):
    ctx, fsdp = mesh.devices.shape
    laid = Mesh(mesh.devices.reshape(RING, ctx // RING, fsdp // 2, 2), AXES)
    rows = P(AXES, None)
    line = P(AXES)
    return jax.shard_map(
        body,
        mesh=laid,
        in_specs=(rows,) * 9 + (line,) * 4,
        out_specs=(rows,) * 9 + (line,) * 4,
        check_vma=False,
    )
```

```python
import jax
import jax.numpy as jnp
from jax import lax
from jax.experimental import pallas as pl
from jax.experimental.pallas import tpu as pltpu
from jax.sharding import Mesh
from jax.sharding import PartitionSpec as P

HEADS = 8
KV_HEADS = 4
HEAD = 256
WINDOW = 4096
CAP = 10.0
EPS = 1e-06
SCALE = HEAD**-0.5
BLOCK = 256

RING = 4
AXES = ("z", "b", "y", "c")
GROUP = ("z", "c")
COPIES = ("b", "y")

bf16 = jnp.bfloat16
f32 = jnp.float32


def swapped(value, axis):
    return lax.ppermute(value, axis, [(0, 1), (1, 0)])


def rotated(value, axis, steps):
    count = lax.axis_size(axis)
    return lax.ppermute(value, axis, [(i, (i + steps) % count) for i in range(count)])


def copies_apart():
    return [(k, j) for k in range(lax.axis_size("b")) for j in range(lax.axis_size("y"))]


def moved_on(value, k, j, back=False):
    if k == 0 and j == 0:
        return value
    count_b, count_y = lax.axis_size("b"), lax.axis_size("y")
    pairs = [
        (b * count_y + y, (b + k) % count_b * count_y + (y + j) % count_y)
        for b in range(count_b)
        for y in range(count_y)
    ]
    return lax.ppermute(value, COPIES, [(t, f) if back else (f, t) for f, t in pairs])


def join(*values):
    return lax.optimization_barrier(values)


def dot_nn(left, right):
    return lax.dot_general(left, right, (((1,), (0,)), ((), ())), preferred_element_type=f32)


def dot_nt(left, right):
    return lax.dot_general(left, right, (((1,), (1,)), ((), ())), preferred_element_type=f32)


def dot_tn(left, right):
    return lax.dot_general(left, right, (((0,), (0,)), ((), ())), preferred_element_type=f32)


def moved(values, first, second):
    rest = values.shape[1] // (first * second)
    starts = [(i * second + j) * rest for j in range(second) for i in range(first)]
    return jnp.concatenate([values[:, s : s + rest] for s in starts], axis=1)


def copies_first(values, normed=False):
    rows, width = values.shape
    copies = lax.axis_size("b") * lax.axis_size("y")

    def kernel(in_ref, out_ref, *normed_refs):
        here = moved(in_ref[...].astype(f32), RING, copies)
        out_ref[...] = here.astype(out_ref.dtype)
        if normed:
            inverse = lax.rsqrt(jnp.mean(here * here, axis=1, keepdims=True) + EPS)
            normed_refs[0][...] = (here * inverse).astype(bf16)
            normed_refs[1][...] = inverse

    out_shape = [jax.ShapeDtypeStruct((rows, width), values.dtype)]
    if normed:
        out_shape.append(jax.ShapeDtypeStruct((rows, width), bf16))
        out_shape.append(jax.ShapeDtypeStruct((rows, 1), f32))
    result = pl.pallas_call(
        kernel,
        out_shape=out_shape,
        compiler_params=pltpu.CompilerParams(vmem_limit_bytes=24 << 20),
        cost_estimate=pl.CostEstimate(
            flops=rows * width, bytes_accessed=8 * rows * width, transcendentals=0
        ),
        name="copies_first",
    )(values)
    return result if normed else result[0]


def copies_back(values):
    rows, width = values.shape
    copies = lax.axis_size("b") * lax.axis_size("y")

    def kernel(in_ref, out_ref):
        out_ref[...] = moved(in_ref[...].astype(f32), copies, RING).astype(out_ref.dtype)

    return pl.pallas_call(
        kernel,
        out_shape=jax.ShapeDtypeStruct((rows, width), values.dtype),
        compiler_params=pltpu.CompilerParams(vmem_limit_bytes=24 << 20),
        cost_estimate=pl.CostEstimate(
            flops=rows * width, bytes_accessed=8 * rows * width, transcendentals=0
        ),
        name="copies_back",
    )(values)


def round_ring(value):
    pairs = [(2 * i, (i + 1) % RING * 2) for i in range(RING)]
    pairs += [(2 * i + 1, (i - 1) % RING * 2 + 1) for i in range(RING)]
    return lax.ppermute(value, GROUP, pairs)


def gather_tokens(own, work=None, beside=(None, None, None)):
    here = own
    chunks, results = [jnp.concatenate([own, swapped(own, "c")], axis=0)], []
    beside = list(beside)
    for step in range(RING):
        results.append(work(step, chunks[step]) if work else ())
        if step == RING - 1:
            return chunks, results, beside
        here = round_ring(here)
        extra = beside[step] or ()
        if results[step] or extra:
            here, results[step], beside[step] = join(here, results[step], extra)
        chunks.append(jnp.concatenate([here, swapped(here, "c")], axis=0))


def relative_places():
    place = None
    for axis in AXES:
        count = lax.axis_size(axis)
        at = (lax.axis_index(axis) - jnp.arange(count, dtype=jnp.int32)) % count
        place = at if place is None else (place[:, None] * count + at[None, :]).reshape(-1)
    return place


def gather_small(value):
    for axis in AXES[::-1]:
        parts = [value] + [rotated(value, axis, k) for k in range(1, lax.axis_size(axis))]
        value = jnp.concatenate(parts, axis=0)
    place = relative_places()
    chosen = place[None, :] == jnp.arange(place.shape[0], dtype=jnp.int32)[:, None]
    return dot_nn(chosen.astype(value.dtype), value)


def scatter_small(value):
    place = relative_places()
    chosen = place[:, None] == jnp.arange(place.shape[0], dtype=jnp.int32)[None, :]
    value = jnp.dot(
        chosen.astype(f32), value, precision=lax.Precision.HIGHEST, preferred_element_type=f32
    )
    for axis in AXES:
        count = lax.axis_size(axis)
        parts = value.reshape(count, -1, value.shape[1])
        total = parts[0]
        for k in range(1, count):
            total = total + rotated(parts[k], axis, -k)
        value = total
    return value[0]


def scatter_tokens(chunks, beside=(None, None, None)):
    rows = chunks[0].shape[0] // 2
    carried = None
    beside = list(beside)
    for step in range(RING):
        chunk = chunks[(step + 1) % RING]
        here = chunk[:rows].astype(f32) + swapped(chunk[rows:], "c").astype(f32)
        if carried is not None:
            here = here + carried.astype(f32)
        if step == RING - 1:
            return here, beside
        carried = round_ring(here.astype(bf16))
        if callable(beside[step]):
            beside[step] = beside[step](beside[step - 1])
        if beside[step] is not None:
            carried, *beside[step] = join(carried, *beside[step])


def exchange(blocks):
    return lax.all_to_all(blocks, GROUP, split_axis=0, concat_axis=0, tiled=True)


def gather_rows(blocks):
    parts, rows, cols = blocks.shape
    return lax.all_gather(blocks.reshape(parts * rows, cols), COPIES, axis=0, tiled=True)


def scatter_rows(grad):
    total = lax.psum_scatter(grad, COPIES, scatter_dimension=0, tiled=True)
    return total.reshape(8, -1, grad.shape[1])


def split_cols(weight):
    rows, cols = weight.shape
    return weight.reshape(rows, 8, cols // 8).transpose(1, 0, 2)


def join_cols(blocks):
    parts, rows, cols = blocks.shape
    return blocks.transpose(1, 0, 2).reshape(rows, parts * cols)


def attention_forward(q, kv_mine, kv_other, meta, run):
    tokens = q.shape[0]
    keys = kv_mine.shape[0]
    block = 2 * run
    q_runs = tokens // run
    steps = tokens // block

    def kernel(meta_ref, q_ref, mine_ref, other_ref, o_ref, lse_ref, acc_ref, sum_ref):
        i = pl.program_id(0)
        core = meta_ref[0]
        q_lows = [meta_ref[1 + 2 * i], meta_ref[2 + 2 * i]]
        acc_ref[...] = jnp.zeros_like(acc_ref)
        sum_ref[...] = jnp.zeros_like(sum_ref)
        lane = lax.broadcasted_iota(jnp.int32, (1, block), 1)
        row = lax.broadcasted_iota(jnp.int32, (block, 1), 0)
        q_pos = row + jnp.where(row < run, q_lows[0], q_lows[1] - run)

        def step(j, carry):
            one = meta_ref[1 + q_runs + 2 * j]
            two = meta_ref[2 + q_runs + 2 * j]

            used = [
                (q_low + run > low) & (q_low - (low + run) < WINDOW)
                for q_low in q_lows
                for low in (one, two)
            ]

            @pl.when(used[0] | used[1] | used[2] | used[3])
            def _():
                place = pl.ds(pl.multiple_of(j * block, block), block)
                mine, other = mine_ref[place, :], other_ref[place, :]
                key = jnp.where(core == 0, mine, other)
                value = jnp.where(core == 0, other, mine)
                scores = dot_nt(q_ref[...], key)
                turned = jnp.tanh(scores * (SCALE / CAP))
                k_pos = lane + jnp.where(lane < run, one, two - run)
                away = q_pos - k_pos
                weight = jnp.where((away >= 0) & (away < WINDOW), jnp.exp(turned * CAP), 0.0)
                sum_ref[...] += jnp.sum(weight, axis=1, keepdims=True)
                acc_ref[...] += dot_nn(weight.astype(bf16), value)

            return carry

        lax.fori_loop(0, keys // block, step, 0)
        total = sum_ref[...]
        o_ref[...] = acc_ref[...] / total
        lse_ref[...] = jnp.log(total)

    return pl.pallas_call(
        kernel,
        grid=(steps,),
        in_specs=[
            pl.BlockSpec(memory_space=pltpu.SMEM),
            pl.BlockSpec((block, HEAD), lambda i: (i, 0)),
            pl.BlockSpec(memory_space=pltpu.VMEM),
            pl.BlockSpec(memory_space=pltpu.VMEM),
        ],
        out_specs=[
            pl.BlockSpec((block, HEAD), lambda i: (i, 0)),
            pl.BlockSpec((block, 1), lambda i: (i, 0)),
        ],
        out_shape=[
            jax.ShapeDtypeStruct((tokens, HEAD), f32),
            jax.ShapeDtypeStruct((tokens, 1), f32),
        ],
        scratch_shapes=[pltpu.VMEM((block, HEAD), f32), pltpu.VMEM((block, 1), f32)],
        compiler_params=pltpu.CompilerParams(vmem_limit_bytes=4 * kv_mine.size + (12 << 20)),
        cost_estimate=pl.CostEstimate(
            flops=4 * tokens * keys * HEAD,
            bytes_accessed=4 * kv_mine.size + 8 * tokens * HEAD,
            transcendentals=2 * tokens * keys,
        ),
        name="attention_forward",
    )(meta, q, kv_mine, kv_other)


def attention_backward(q, d_out, kv_mine, kv_other, meta, lse, delta, run):
    tokens = q.shape[0]
    keys = kv_mine.shape[0]
    q_block = 2 * run
    block_k = 2 * run
    steps = tokens // q_block
    key_steps = keys // block_k
    q_runs, last = tokens // run, keys // run - 1

    def kernel(
        meta_ref, q_ref, d_ref, mine_ref, other_ref, lse_ref, delta_ref,
        dq_ref, d_mine_ref, d_other_ref, key_acc, value_acc, key_ref, value_ref,
    ):
        j = pl.program_id(0)
        core = meta_ref[0]
        at = j * block_k
        one = at // run
        two = jnp.minimum((at + block_k - 1) // run, last)
        one_pos = meta_ref[1 + q_runs + one] + at - one * run
        two_pos = meta_ref[1 + q_runs + two] + at - two * run
        turn_at = jnp.minimum((one + 1) * run - at, block_k)
        row = lax.broadcasted_iota(jnp.int32, (block_k, 1), 0)
        k_pos = row + jnp.where(row < turn_at, one_pos, two_pos)
        k_runs = [(one_pos, turn_at), (two_pos + turn_at, block_k - turn_at)]

        @pl.when(j == 0)
        def _():
            dq_ref[...] = jnp.zeros_like(dq_ref)

        key_acc[...] = jnp.zeros_like(key_acc)
        value_acc[...] = jnp.zeros_like(value_acc)
        key_ref[...] = jnp.where(core == 0, mine_ref[...], other_ref[...])
        value_ref[...] = jnp.where(core == 0, other_ref[...], mine_ref[...])
        for i in range(steps):
            q_runs_here = []
            first = i * q_block
            while first < (i + 1) * q_block:
                number = first // run
                stop = min((number + 1) * run, (i + 1) * q_block)
                q_runs_here.append((first, stop, meta_ref[1 + number] - number * run))
                first = stop
            used = None
            for first, stop, q_shift in q_runs_here:
                for low, size in k_runs:
                    here = (q_shift + stop > low) & (q_shift + first - (low + size) < WINDOW)
                    here = here & (size > 0)
                    used = here if used is None else used | here

            @pl.when(used)
            def _(i=i, q_runs_here=q_runs_here):
                place = pl.ds(i * q_block, q_block)
                key = key_ref[...]
                value = value_ref[...]
                query = q_ref[place, :]
                d_here = d_ref[place, :]
                turned = jnp.tanh(dot_nt(key, query) * (SCALE / CAP))
                lane = lax.broadcasted_iota(jnp.int32, (1, q_block), 1) + i * q_block
                q_pos = lane + q_runs_here[-1][2]
                for first, stop, q_shift in q_runs_here[-2::-1]:
                    q_pos = jnp.where(lane < stop, lane + q_shift, q_pos)
                away = q_pos - k_pos
                soft = jnp.where(
                    (away >= 0) & (away < WINDOW),
                    jnp.exp(turned * CAP - lse_ref[:, place]),
                    0.0,
                )
                d_prob = dot_nt(value, d_here)
                d_raw = soft * (d_prob - delta_ref[:, place]) * (1.0 - turned * turned)
                d_raw = d_raw.astype(bf16)
                value_acc[...] += dot_nn(soft.astype(bf16), d_here)
                key_acc[...] += dot_nn(d_raw, query)
                dq_ref[place, :] += dot_tn(d_raw, key)

        d_key, d_value = (key_acc[...] * SCALE).astype(bf16), value_acc[...].astype(bf16)
        d_mine_ref[...] = jnp.where(core == 0, d_key, d_value)
        d_other_ref[...] = jnp.where(core == 0, d_value, d_key)

        @pl.when(j == key_steps - 1)
        def _():
            dq_ref[...] = dq_ref[...] * SCALE

    whole = pl.BlockSpec(memory_space=pltpu.VMEM)
    block = pl.BlockSpec((block_k, HEAD), lambda j: (j, 0))
    return pl.pallas_call(
        kernel,
        grid=(key_steps,),
        in_specs=[
            pl.BlockSpec(memory_space=pltpu.SMEM),
            whole,
            whole,
            block,
            block,
            whole,
            whole,
        ],
        out_specs=[whole, block, block],
        out_shape=[
            jax.ShapeDtypeStruct((tokens, HEAD), f32),
            jax.ShapeDtypeStruct((keys, HEAD), bf16),
            jax.ShapeDtypeStruct((keys, HEAD), bf16),
        ],
        scratch_shapes=[
            pltpu.VMEM((block_k, HEAD), f32),
            pltpu.VMEM((block_k, HEAD), f32),
            pltpu.VMEM((block_k, HEAD), bf16),
            pltpu.VMEM((block_k, HEAD), bf16),
        ],
        compiler_params=pltpu.CompilerParams(vmem_limit_bytes=24 << 20),
        cost_estimate=pl.CostEstimate(
            flops=10 * tokens * keys * HEAD,
            bytes_accessed=8 * kv_mine.size + 8 * tokens * HEAD,
            transcendentals=2 * tokens * keys,
        ),
        name="attention_backward",
    )(meta, q, d_out, kv_mine, kv_other, lse, delta)


def rotated_halves(values, cosine, sine):
    half = HEAD // 2
    a, b = values[:, :half], values[:, half:]
    return jnp.concatenate([a * cosine - b * sine, b * cosine + a * sine], axis=1)


BACK = [0] + list(range(RING - 1, 0, -1))


def call_on_rows(kernel, name, out_shape, *operands):
    size = sum(x.size * x.dtype.itemsize for x in operands)
    return pl.pallas_call(
        kernel,
        in_specs=[pl.BlockSpec(memory_space=pltpu.SMEM)]
        + [pl.BlockSpec(memory_space=pltpu.VMEM)] * (len(operands) - 1),
        out_shape=out_shape,
        compiler_params=pltpu.CompilerParams(vmem_limit_bytes=24 << 20),
        cost_estimate=pl.CostEstimate(flops=size, bytes_accessed=2 * size, transcendentals=0),
        name=name,
    )(*operands)


def to_blocks(chunks, core, tables=None):
    tok, width = chunks[0].shape[0] // 2, chunks[0].shape[1]
    heads = width // HEAD

    def kernel(core_ref, *refs):
        first = core_ref[0] == 0
        outs = refs[-heads:]
        for d in range(RING):
            for e in range(2):
                one = refs[BACK[d] if e else d][e * tok : (e + 1) * tok, :]
                two = refs[BACK[d] if e else d][(1 - e) * tok : (2 - e) * tok, :]
                here = jnp.where(first, one, two)
                place = pl.ds((2 * d + e) * tok, tok)
                for h in range(heads):
                    part = here[:, h * HEAD : (h + 1) * HEAD]
                    if tables is not None:
                        cosine, sine = refs[RING][place, :], refs[RING + 1][place, :]
                        turned = rotated_halves(part, cosine, sine)
                        part = jnp.where(first, turned, part) if h else turned
                    outs[h][place, :] = part.astype(bf16)

    shape = jax.ShapeDtypeStruct((2 * RING * tok, HEAD), bf16)
    return call_on_rows(kernel, "to_blocks", [shape] * heads, core, *chunks, *(tables or ()))


def to_chunks(values, core, tables=None, keyed=False):
    tok = values.shape[0] // (2 * RING)

    def kernel(core_ref, *refs):
        first = core_ref[0] == 0
        for s in range(RING):
            for p in range(2):
                parts = []
                for d, e in ((BACK[s] if p else s, p), (s if p else BACK[s], 1 - p)):
                    place = pl.ds((2 * d + e) * tok, tok)
                    part = refs[0][place, :]
                    if tables is not None:
                        cosine, sine = refs[1][place, :], refs[2][place, :]
                        turned = rotated_halves(part, cosine, -sine)
                        part = jnp.where(first, turned, part) if keyed else turned
                    parts.append(part)
                here = jnp.where(first, parts[0], parts[1])
                refs[-1][pl.ds((2 * s + p) * tok, tok), :] = here.astype(bf16)

    shape = jax.ShapeDtypeStruct(values.shape, bf16)
    return call_on_rows(kernel, "to_chunks", shape, core, values, *(tables or ()))


def mean(values):
    return jnp.mean(values, axis=1, keepdims=True)


def gelu_parts(u):
    k = 0.7978845608028654
    t = jnp.tanh(k * (u + 0.044715 * u * u * u))
    value = 0.5 * u * (1.0 + t)
    slope = 0.5 * (1.0 + t) + 0.5 * u * (1.0 - t * t) * k * (1.0 + 3 * 0.044715 * u * u)
    return value, slope


def body(
    inputs,
    cotangent,
    w_query,
    w_key,
    w_value,
    w_out_t,
    w_gate,
    w_up,
    w_down_t,
    gain_attn_in,
    gain_attn_out,
    gain_mlp_in,
    gain_mlp_out,
):
    tok, width = inputs.shape
    rows = w_query.shape[0]
    count_b, count_y = lax.axis_size("b"), lax.axis_size("y")
    z, b, y, c = [lax.axis_index(name) for name in AXES]

    g_attn = gain_attn_in.astype(f32)[:, None]
    g_mlp = gain_mlp_in.astype(f32)[:, None]

    def scaled(weight, gain):
        return (weight.astype(f32) * gain).astype(bf16)

    pairs = jnp.stack(
        [w_key.reshape(rows, KV_HEADS, HEAD), w_value.reshape(rows, KV_HEADS, HEAD)], axis=2
    ).reshape(rows, 8, HEAD)
    qkv_pack = jnp.concatenate([w_query.reshape(rows, 8, HEAD), pairs], axis=2)
    qkv_pack = (qkv_pack.astype(f32) * g_attn[:, :, None]).astype(bf16)
    qkv_pack = jnp.concatenate([qkv_pack, w_out_t.reshape(rows, 8, HEAD)], axis=2)
    qkv_pack = qkv_pack.transpose(1, 0, 2)
    x, normed_x, r1 = copies_first(inputs, normed=True)
    x = x.astype(f32)
    gate_pack = split_cols(scaled(w_gate, g_mlp))
    up_pack = split_cols(scaled(w_up, g_mlp))
    down_pack = split_cols(w_down_t)
    qkv_w = gather_rows(exchange(qkv_pack))
    qkv_w, out_w = qkv_w[:, : 2 * HEAD], qkv_w[:, 2 * HEAD :]
    gains = jnp.concatenate([gain_attn_out, gain_mlp_out])[None]
    gains = gather_small(gains)
    x1, _, (_, _, (gate_pack,)) = gather_tokens(normed_x, None, (None, None, (gate_pack,)))
    gate_mine = exchange(gate_pack)
    qkv = [dot_nn(part, qkv_w) for part in x1]
    run = 2 * tok

    def starts(places_b, places_y):
        blocks = (z - jnp.arange(RING, dtype=jnp.int32)) % RING
        place = (blocks * count_b + places_b[:, None, None]) * count_y + places_y[:, None]
        return place.reshape(-1) * run

    q_starts = starts(b[None], y[None])
    k_starts = starts(
        (b - jnp.arange(count_b, dtype=jnp.int32)) % count_b,
        (y - jnp.arange(count_y, dtype=jnp.int32)) % count_y,
    )
    meta = jnp.concatenate([c.astype(jnp.int32)[None], q_starts, k_starts])

    core = c.astype(jnp.int32)[None]
    q_pos = (q_starts[:, None] + jnp.arange(run, dtype=jnp.int32)).reshape(-1)
    frequency = 10000.0 ** (-jnp.arange(HEAD // 2, dtype=f32) * 2.0 / HEAD)
    angles = q_pos.astype(f32)[:, None] * frequency[None, :]
    tables = (jnp.cos(angles), jnp.sin(angles))

    q, own_kv = to_blocks(qkv, core, tables)
    kv_mine = jnp.concatenate([moved_on(own_kv, k, j) for k, j in copies_apart()], axis=0)
    kv_mine, gate_mine, up_pack, gains = join(kv_mine, gate_mine, up_pack, gains)
    gate_w = gather_rows(gate_mine)
    up_mine = exchange(up_pack)
    kv_other = swapped(kv_mine, "c")
    attended, lse = attention_forward(q, kv_mine, kv_other, meta, run)
    attended, up_mine, down_pack = join(attended, up_mine, down_pack)
    up_w = gather_rows(up_mine)
    down_mine = exchange(down_pack)
    g_attn_out = moved(gains[:, :rows].reshape(1, width), RING, count_b * count_y)
    g_mlp_out = moved(gains[:, rows:].reshape(1, width), RING, count_b * count_y)
    attended_b = to_chunks(attended, core)
    size = 2 * tok

    def cut(values):
        return [values[i * size : (i + 1) * size] for i in range(RING)]

    projected, ((gate_w,), (down_mine,), _) = scatter_tokens(
        [dot_nt(part, out_w).astype(bf16) for part in cut(attended_b)],
        ((gate_w,), (down_mine,), None),
    )
    down_w = gather_rows(down_mine)
    r2 = lax.rsqrt(mean(projected * projected) + EPS)
    hidden = x + projected * r2 * g_attn_out

    r3 = lax.rsqrt(mean(hidden * hidden) + EPS)
    def mlp_forward(i, part):
        gate = dot_nn(part, gate_w).astype(bf16)
        up = dot_nn(part, up_w).astype(bf16)
        return gate, up, (gelu_parts(gate.astype(f32))[0] * up.astype(f32)).astype(bf16)

    x2, mlp, _ = gather_tokens((hidden * r3).astype(bf16), mlp_forward)
    gate, up, mixed = zip(*mlp)
    *x1, hidden = join(*x1, hidden)
    x1, x2, all_mixed = [jnp.concatenate(parts, axis=0) for parts in (x1, x2, mixed)]
    reduced, ((x2,), (x1, all_mixed), _) = scatter_tokens(
        [dot_nt(part, down_w).astype(bf16) for part in mixed], ((x2,), (x1, all_mixed), None)
    )
    r4 = lax.rsqrt(mean(reduced * reduced) + EPS)

    top = copies_first(cotangent).astype(f32)
    lifted = top * g_mlp_out
    d_reduced = r4 * lifted - reduced * (r4 * r4 * r4 * mean(lifted * reduced))
    def mlp_backward(i, part):
        d_mixed = dot_nn(part, down_w)
        gelu, slope = gelu_parts(gate[i].astype(f32))
        d_gate = (d_mixed * up[i].astype(f32) * slope).astype(bf16)
        d_up = (d_mixed * gelu).astype(bf16)
        return d_gate, d_up, (dot_nt(d_gate, gate_w) + dot_nt(d_up, up_w)).astype(bf16)

    x3, mlp, _ = gather_tokens(d_reduced.astype(bf16), mlp_backward)
    d_gate, d_up, dn3 = zip(*mlp)
    x3 = jnp.concatenate(x3, axis=0)
    down_part = dot_tn(x3, all_mixed).astype(bf16)
    gate_part = dot_tn(x2, jnp.concatenate(d_gate, axis=0)).astype(bf16)
    up_part = dot_tn(x2, jnp.concatenate(d_up, axis=0)).astype(bf16)
    dn3, ((down_part,), (gate_part,), (up_part,)) = scatter_tokens(
        dn3, ((down_part,), (gate_part,), (up_part,))
    )
    down_rows, gate_rows, up_rows = [scatter_rows(p) for p in (down_part, gate_part, up_part)]
    d_hidden = top + r3 * dn3 - hidden * (r3 * r3 * r3 * mean(dn3 * hidden))
    lifted = d_hidden * g_attn_out
    d_projected = r2 * lifted - projected * (r2 * r2 * r2 * mean(lifted * projected))
    d_projected, d_hidden, reduced = join(d_projected.astype(bf16), d_hidden, reduced)
    output = copies_back((hidden + reduced * r4 * g_mlp_out).astype(bf16))
    d_gain_mlp_out = jnp.sum(top * reduced * r4, axis=0, keepdims=True)
    d_gain_attn_out = jnp.sum(d_hidden * projected * r2, axis=0, keepdims=True)
    d_gains = jnp.concatenate(
        [
            moved(d_gain_attn_out, count_b * count_y, RING).reshape(-1, rows),
            moved(d_gain_mlp_out, count_b * count_y, RING).reshape(-1, rows),
        ],
        axis=1,
    )
    d_gains = scatter_small(d_gains)
    x4, d_attended, ((output,), _, _) = gather_tokens(
        d_projected, lambda i, part: (dot_nn(part, out_w).astype(bf16),), ((output,), None, None)
    )
    (d_attended,) = to_blocks([part[0] for part in d_attended], core)
    delta = jnp.sum(d_attended.astype(f32) * attended, axis=1)
    delta, down_rows, gate_rows, d_gains = join(delta, down_rows, gate_rows, d_gains)
    down_sum = exchange(down_rows)
    d_query, d_mine, d_other = attention_backward(
        q, d_attended, kv_mine, kv_other, meta, lse.reshape(1, -1), delta[None], run
    )
    d_query, d_mine, d_other, down_sum, gate_rows = join(
        d_query, d_mine, d_other, down_sum, gate_rows
    )
    gate_sum = exchange(gate_rows)
    d_mine = (d_mine.astype(f32) + swapped(d_other, "c").astype(f32)).astype(bf16)
    d_parts = d_mine.reshape(count_b * count_y, -1, HEAD)
    d_own = sum(
        moved_on(part, k, j, back=True).astype(f32) for part, (k, j) in zip(d_parts, copies_apart())
    )
    d_own, d_query, *x4, gate_sum, up_rows = join(d_own, d_query, *x4, gate_sum, up_rows)
    up_sum = exchange(up_rows)
    d_q = to_chunks(d_query, core, tables)
    d_k = to_chunks(d_own, core, tables, keyed=True)
    d_qkv = jnp.concatenate([d_q, d_k], axis=1)
    q_part = dot_tn(x1, d_q)
    out_part = dot_tn(jnp.concatenate(x4, axis=0), attended_b)
    kv_part = dot_tn(x1, d_k)
    attn_part = jnp.concatenate([q_part, out_part, kv_part], axis=1).astype(bf16)
    d_qkv, attn_part = join(d_qkv, attn_part)
    attn_rows = scatter_rows(attn_part)
    dn1, (_, (up_sum, _), (attn_sum,)) = scatter_tokens(
        [dot_nt(part, qkv_w).astype(bf16) for part in cut(d_qkv)],
        (None, (up_sum, attn_rows), lambda before: (exchange(before[1]),)),
    )
    down_sum, gate_sum, up_sum, attn_sum = [
        part.astype(f32) for part in (down_sum, gate_sum, up_sum, attn_sum)
    ]
    q_sum, out_sum, kv_sum = [attn_sum[:, :, i * HEAD : (i + 1) * HEAD] for i in range(3)]
    q_sum, out_sum = join_cols(q_sum), join_cols(out_sum)
    kv_sum = kv_sum.reshape(KV_HEADS, 2, rows, HEAD)
    d_source = r1 * dn1 - x * (r1 * r1 * r1 * mean(dn1 * x))
    input_grad = copies_back((d_hidden + d_source).astype(bf16))

    k_sum, v_sum = join_cols(kv_sum[:, 0]), join_cols(kv_sum[:, 1])
    gate_sum, up_sum = join_cols(gate_sum), join_cols(up_sum)

    def row_term(weight, grad):
        return jnp.sum(weight.astype(f32) * grad, axis=1)

    d_gain_attn_in = (
        row_term(w_query, q_sum) + row_term(w_key, k_sum) + row_term(w_value, v_sum)
    )
    d_gain_mlp_in = row_term(w_gate, gate_sum) + row_term(w_up, up_sum)
    return (
        output,
        input_grad,
        q_sum * g_attn,
        k_sum * g_attn,
        v_sum * g_attn,
        out_sum,
        gate_sum * g_mlp,
        up_sum * g_mlp,
        join_cols(down_sum),
        d_gain_attn_in,
        d_gains[:rows],
        d_gain_mlp_in,
        d_gains[rows:],
    )


def solution(mesh):
    ctx, fsdp = mesh.devices.shape
    laid = Mesh(mesh.devices.reshape(RING, ctx // RING, fsdp // 2, 2), AXES)
    rows = P(AXES, None)
    line = P(AXES)
    return jax.shard_map(
        body,
        mesh=laid,
        in_specs=(rows,) * 9 + (line,) * 4,
        out_specs=(rows,) * 9 + (line,) * 4,
        check_vma=False,
    )
```

```python
import jax
import jax.numpy as jnp
from jax import lax
from jax.experimental import pallas as pl
from jax.experimental.pallas import tpu as pltpu
from jax.sharding import Mesh
from jax.sharding import PartitionSpec as P

HEADS = 8
KV_HEADS = 4
HEAD = 256
WINDOW = 4096
CAP = 10.0
EPS = 1e-06
SCALE = HEAD**-0.5
BLOCK = 256

RING = 4
AXES = ("z", "b", "y", "c")
GROUP = ("z", "c")
COPIES = ("b", "y")

bf16 = jnp.bfloat16
f32 = jnp.float32


def swapped(value, axis):
    return lax.ppermute(value, axis, [(0, 1), (1, 0)])


def rotated(value, axis, steps):
    count = lax.axis_size(axis)
    return lax.ppermute(value, axis, [(i, (i + steps) % count) for i in range(count)])


def copies_apart():
    return [(k, j) for k in range(lax.axis_size("b")) for j in range(lax.axis_size("y"))]


def moved_on(value, k, j, back=False):
    if k == 0 and j == 0:
        return value
    count_b, count_y = lax.axis_size("b"), lax.axis_size("y")
    pairs = [
        (b * count_y + y, (b + k) % count_b * count_y + (y + j) % count_y)
        for b in range(count_b)
        for y in range(count_y)
    ]
    return lax.ppermute(value, COPIES, [(t, f) if back else (f, t) for f, t in pairs])


def join(*values):
    return lax.optimization_barrier(values)


def dot_nn(left, right):
    return lax.dot_general(left, right, (((1,), (0,)), ((), ())), preferred_element_type=f32)


def dot_nt(left, right):
    return lax.dot_general(left, right, (((1,), (1,)), ((), ())), preferred_element_type=f32)


def dot_tn(left, right):
    return lax.dot_general(left, right, (((0,), (0,)), ((), ())), preferred_element_type=f32)


def moved(values, first, second):
    rest = values.shape[1] // (first * second)
    starts = [(i * second + j) * rest for j in range(second) for i in range(first)]
    return jnp.concatenate([values[:, s : s + rest] for s in starts], axis=1)


def copies_first(values, normed=False):
    rows, width = values.shape
    copies = lax.axis_size("b") * lax.axis_size("y")

    def kernel(in_ref, out_ref, *normed_refs):
        here = moved(in_ref[...].astype(f32), RING, copies)
        out_ref[...] = here.astype(out_ref.dtype)
        if normed:
            inverse = lax.rsqrt(jnp.mean(here * here, axis=1, keepdims=True) + EPS)
            normed_refs[0][...] = (here * inverse).astype(bf16)
            normed_refs[1][...] = inverse

    out_shape = [jax.ShapeDtypeStruct((rows, width), values.dtype)]
    if normed:
        out_shape.append(jax.ShapeDtypeStruct((rows, width), bf16))
        out_shape.append(jax.ShapeDtypeStruct((rows, 1), f32))
    result = pl.pallas_call(
        kernel,
        out_shape=out_shape,
        compiler_params=pltpu.CompilerParams(vmem_limit_bytes=24 << 20),
        cost_estimate=pl.CostEstimate(
            flops=rows * width, bytes_accessed=8 * rows * width, transcendentals=0
        ),
        name="copies_first",
    )(values)
    return result if normed else result[0]


def copies_back(values):
    rows, width = values.shape
    copies = lax.axis_size("b") * lax.axis_size("y")

    def kernel(in_ref, out_ref):
        out_ref[...] = moved(in_ref[...].astype(f32), copies, RING).astype(out_ref.dtype)

    return pl.pallas_call(
        kernel,
        out_shape=jax.ShapeDtypeStruct((rows, width), values.dtype),
        compiler_params=pltpu.CompilerParams(vmem_limit_bytes=24 << 20),
        cost_estimate=pl.CostEstimate(
            flops=rows * width, bytes_accessed=8 * rows * width, transcendentals=0
        ),
        name="copies_back",
    )(values)


def round_ring(value):
    pairs = [(2 * i, (i + 1) % RING * 2) for i in range(RING)]
    pairs += [(2 * i + 1, (i - 1) % RING * 2 + 1) for i in range(RING)]
    return lax.ppermute(value, GROUP, pairs)


def gather_tokens(own, work=None, beside=(None, None, None)):
    here = own
    chunks, results = [jnp.concatenate([own, swapped(own, "c")], axis=0)], []
    beside = list(beside)
    for step in range(RING):
        results.append(work(step, chunks[step]) if work else ())
        if step == RING - 1:
            return chunks, results, beside
        here = round_ring(here)
        extra = beside[step] or ()
        if results[step] or extra:
            here, results[step], beside[step] = join(here, results[step], extra)
        chunks.append(jnp.concatenate([here, swapped(here, "c")], axis=0))


def relative_places():
    place = None
    for axis in AXES:
        count = lax.axis_size(axis)
        at = (lax.axis_index(axis) - jnp.arange(count, dtype=jnp.int32)) % count
        place = at if place is None else (place[:, None] * count + at[None, :]).reshape(-1)
    return place


def gather_small(value):
    for axis in AXES[::-1]:
        parts = [value] + [rotated(value, axis, k) for k in range(1, lax.axis_size(axis))]
        value = jnp.concatenate(parts, axis=0)
    place = relative_places()
    chosen = place[None, :] == jnp.arange(place.shape[0], dtype=jnp.int32)[:, None]
    return dot_nn(chosen.astype(value.dtype), value)


def scatter_small(value):
    place = relative_places()
    chosen = place[:, None] == jnp.arange(place.shape[0], dtype=jnp.int32)[None, :]
    value = jnp.dot(
        chosen.astype(f32), value, precision=lax.Precision.HIGHEST, preferred_element_type=f32
    )
    for axis in AXES:
        count = lax.axis_size(axis)
        parts = value.reshape(count, -1, value.shape[1])
        total = parts[0]
        for k in range(1, count):
            total = total + rotated(parts[k], axis, -k)
        value = total
    return value[0]


def scatter_tokens(chunks, beside=(None, None, None), first=()):
    rows = chunks[0].shape[0] // 2
    carried = None
    beside = list(beside)
    for step in range(RING):
        chunk = chunks[(step + 1) % RING]
        here = chunk[:rows].astype(f32) + swapped(chunk[rows:], "c").astype(f32)
        if carried is not None:
            here = here + carried.astype(f32)
        if step == RING - 1:
            return here, beside
        if step == 0 and first:
            here, *first = join(here, *first)
        carried = round_ring(here.astype(bf16))
        if callable(beside[step]):
            beside[step] = beside[step](beside[step - 1] if step > 1 else first)
        if beside[step] is not None:
            carried, *beside[step] = join(carried, *beside[step])


def exchange(blocks):
    return lax.all_to_all(blocks, GROUP, split_axis=0, concat_axis=0, tiled=True)


def gather_rows(blocks):
    parts, rows, cols = blocks.shape
    return lax.all_gather(blocks.reshape(parts * rows, cols), COPIES, axis=0, tiled=True)


def scatter_rows(grad):
    total = lax.psum_scatter(grad, COPIES, scatter_dimension=0, tiled=True)
    return total.reshape(8, -1, grad.shape[1])


def split_cols(weight):
    rows, cols = weight.shape
    return weight.reshape(rows, 8, cols // 8).transpose(1, 0, 2)


def join_cols(blocks):
    parts, rows, cols = blocks.shape
    return blocks.transpose(1, 0, 2).reshape(rows, parts * cols)


def attention_forward(q, kv_mine, kv_other, meta, run):
    tokens = q.shape[0]
    keys = kv_mine.shape[0]
    block = 2 * run
    q_runs = tokens // run
    steps = tokens // block

    def kernel(meta_ref, q_ref, mine_ref, other_ref, o_ref, lse_ref, acc_ref, sum_ref):
        i = pl.program_id(0)
        core = meta_ref[0]
        q_lows = [meta_ref[1 + 2 * i], meta_ref[2 + 2 * i]]
        acc_ref[...] = jnp.zeros_like(acc_ref)
        sum_ref[...] = jnp.zeros_like(sum_ref)
        lane = lax.broadcasted_iota(jnp.int32, (1, block), 1)
        row = lax.broadcasted_iota(jnp.int32, (block, 1), 0)
        q_pos = row + jnp.where(row < run, q_lows[0], q_lows[1] - run)

        def step(j, carry):
            one = meta_ref[1 + q_runs + 2 * j]
            two = meta_ref[2 + q_runs + 2 * j]

            used = [
                (q_low + run > low) & (q_low - (low + run) < WINDOW)
                for q_low in q_lows
                for low in (one, two)
            ]

            @pl.when(used[0] | used[1] | used[2] | used[3])
            def _():
                place = pl.ds(pl.multiple_of(j * block, block), block)
                mine, other = mine_ref[place, :], other_ref[place, :]
                key = jnp.where(core == 0, mine, other)
                value = jnp.where(core == 0, other, mine)
                scores = dot_nt(q_ref[...], key)
                turned = jnp.tanh(scores * (SCALE / CAP))
                k_pos = lane + jnp.where(lane < run, one, two - run)
                away = q_pos - k_pos
                weight = jnp.where((away >= 0) & (away < WINDOW), jnp.exp(turned * CAP), 0.0)
                sum_ref[...] += jnp.sum(weight, axis=1, keepdims=True)
                acc_ref[...] += dot_nn(weight.astype(bf16), value)

            return carry

        lax.fori_loop(0, keys // block, step, 0)
        total = sum_ref[...]
        o_ref[...] = acc_ref[...] / total
        lse_ref[...] = jnp.log(total)

    return pl.pallas_call(
        kernel,
        grid=(steps,),
        in_specs=[
            pl.BlockSpec(memory_space=pltpu.SMEM),
            pl.BlockSpec((block, HEAD), lambda i: (i, 0)),
            pl.BlockSpec(memory_space=pltpu.VMEM),
            pl.BlockSpec(memory_space=pltpu.VMEM),
        ],
        out_specs=[
            pl.BlockSpec((block, HEAD), lambda i: (i, 0)),
            pl.BlockSpec((block, 1), lambda i: (i, 0)),
        ],
        out_shape=[
            jax.ShapeDtypeStruct((tokens, HEAD), f32),
            jax.ShapeDtypeStruct((tokens, 1), f32),
        ],
        scratch_shapes=[pltpu.VMEM((block, HEAD), f32), pltpu.VMEM((block, 1), f32)],
        compiler_params=pltpu.CompilerParams(vmem_limit_bytes=4 * kv_mine.size + (12 << 20)),
        cost_estimate=pl.CostEstimate(
            flops=4 * tokens * keys * HEAD,
            bytes_accessed=4 * kv_mine.size + 8 * tokens * HEAD,
            transcendentals=2 * tokens * keys,
        ),
        name="attention_forward",
    )(meta, q, kv_mine, kv_other)


def attention_backward(q, d_out, kv_mine, kv_other, meta, lse, delta, run):
    tokens = q.shape[0]
    keys = kv_mine.shape[0]
    q_block = 2 * run
    block_k = 2 * run
    steps = tokens // q_block
    key_steps = keys // block_k
    q_runs, last = tokens // run, keys // run - 1

    def kernel(
        meta_ref, q_ref, d_ref, mine_ref, other_ref, lse_ref, delta_ref,
        dq_ref, d_mine_ref, d_other_ref, key_acc, value_acc, key_ref, value_ref,
    ):
        j = pl.program_id(0)
        core = meta_ref[0]
        at = j * block_k
        one = at // run
        two = jnp.minimum((at + block_k - 1) // run, last)
        one_pos = meta_ref[1 + q_runs + one] + at - one * run
        two_pos = meta_ref[1 + q_runs + two] + at - two * run
        turn_at = jnp.minimum((one + 1) * run - at, block_k)
        row = lax.broadcasted_iota(jnp.int32, (block_k, 1), 0)
        k_pos = row + jnp.where(row < turn_at, one_pos, two_pos)
        k_runs = [(one_pos, turn_at), (two_pos + turn_at, block_k - turn_at)]

        @pl.when(j == 0)
        def _():
            dq_ref[...] = jnp.zeros_like(dq_ref)

        key_acc[...] = jnp.zeros_like(key_acc)
        value_acc[...] = jnp.zeros_like(value_acc)
        key_ref[...] = jnp.where(core == 0, mine_ref[...], other_ref[...])
        value_ref[...] = jnp.where(core == 0, other_ref[...], mine_ref[...])
        for i in range(steps):
            q_runs_here = []
            first = i * q_block
            while first < (i + 1) * q_block:
                number = first // run
                stop = min((number + 1) * run, (i + 1) * q_block)
                q_runs_here.append((first, stop, meta_ref[1 + number] - number * run))
                first = stop
            used = None
            for first, stop, q_shift in q_runs_here:
                for low, size in k_runs:
                    here = (q_shift + stop > low) & (q_shift + first - (low + size) < WINDOW)
                    here = here & (size > 0)
                    used = here if used is None else used | here

            @pl.when(used)
            def _(i=i, q_runs_here=q_runs_here):
                place = pl.ds(i * q_block, q_block)
                key = key_ref[...]
                value = value_ref[...]
                query = q_ref[place, :]
                d_here = d_ref[place, :]
                turned = jnp.tanh(dot_nt(key, query) * (SCALE / CAP))
                lane = lax.broadcasted_iota(jnp.int32, (1, q_block), 1) + i * q_block
                q_pos = lane + q_runs_here[-1][2]
                for first, stop, q_shift in q_runs_here[-2::-1]:
                    q_pos = jnp.where(lane < stop, lane + q_shift, q_pos)
                away = q_pos - k_pos
                soft = jnp.where(
                    (away >= 0) & (away < WINDOW),
                    jnp.exp(turned * CAP - lse_ref[:, place]),
                    0.0,
                )
                d_prob = dot_nt(value, d_here)
                d_raw = soft * (d_prob - delta_ref[:, place]) * (1.0 - turned * turned)
                d_raw = d_raw.astype(bf16)
                value_acc[...] += dot_nn(soft.astype(bf16), d_here)
                key_acc[...] += dot_nn(d_raw, query)
                dq_ref[place, :] += dot_tn(d_raw, key)

        d_key, d_value = (key_acc[...] * SCALE).astype(bf16), value_acc[...].astype(bf16)
        d_mine_ref[...] = jnp.where(core == 0, d_key, d_value)
        d_other_ref[...] = jnp.where(core == 0, d_value, d_key)

        @pl.when(j == key_steps - 1)
        def _():
            dq_ref[...] = dq_ref[...] * SCALE

    whole = pl.BlockSpec(memory_space=pltpu.VMEM)
    block = pl.BlockSpec((block_k, HEAD), lambda j: (j, 0))
    return pl.pallas_call(
        kernel,
        grid=(key_steps,),
        in_specs=[
            pl.BlockSpec(memory_space=pltpu.SMEM),
            whole,
            whole,
            block,
            block,
            whole,
            whole,
        ],
        out_specs=[whole, block, block],
        out_shape=[
            jax.ShapeDtypeStruct((tokens, HEAD), f32),
            jax.ShapeDtypeStruct((keys, HEAD), bf16),
            jax.ShapeDtypeStruct((keys, HEAD), bf16),
        ],
        scratch_shapes=[
            pltpu.VMEM((block_k, HEAD), f32),
            pltpu.VMEM((block_k, HEAD), f32),
            pltpu.VMEM((block_k, HEAD), bf16),
            pltpu.VMEM((block_k, HEAD), bf16),
        ],
        compiler_params=pltpu.CompilerParams(vmem_limit_bytes=24 << 20),
        cost_estimate=pl.CostEstimate(
            flops=10 * tokens * keys * HEAD,
            bytes_accessed=8 * kv_mine.size + 8 * tokens * HEAD,
            transcendentals=2 * tokens * keys,
        ),
        name="attention_backward",
    )(meta, q, d_out, kv_mine, kv_other, lse, delta)


def rotated_halves(values, cosine, sine):
    half = HEAD // 2
    a, b = values[:, :half], values[:, half:]
    return jnp.concatenate([a * cosine - b * sine, b * cosine + a * sine], axis=1)


BACK = [0] + list(range(RING - 1, 0, -1))


def call_on_rows(kernel, name, out_shape, *operands):
    size = sum(x.size * x.dtype.itemsize for x in operands)
    return pl.pallas_call(
        kernel,
        in_specs=[pl.BlockSpec(memory_space=pltpu.SMEM)]
        + [pl.BlockSpec(memory_space=pltpu.VMEM)] * (len(operands) - 1),
        out_shape=out_shape,
        compiler_params=pltpu.CompilerParams(vmem_limit_bytes=24 << 20),
        cost_estimate=pl.CostEstimate(flops=size, bytes_accessed=2 * size, transcendentals=0),
        name=name,
    )(*operands)


def to_blocks(chunks, core, tables=None):
    tok, width = chunks[0].shape[0] // 2, chunks[0].shape[1]
    heads = width // HEAD

    def kernel(core_ref, *refs):
        first = core_ref[0] == 0
        outs = refs[-heads:]
        for d in range(RING):
            for e in range(2):
                one = refs[BACK[d] if e else d][e * tok : (e + 1) * tok, :]
                two = refs[BACK[d] if e else d][(1 - e) * tok : (2 - e) * tok, :]
                here = jnp.where(first, one, two)
                place = pl.ds((2 * d + e) * tok, tok)
                for h in range(heads):
                    part = here[:, h * HEAD : (h + 1) * HEAD]
                    if tables is not None:
                        cosine, sine = refs[RING][place, :], refs[RING + 1][place, :]
                        turned = rotated_halves(part, cosine, sine)
                        part = jnp.where(first, turned, part) if h else turned
                    outs[h][place, :] = part.astype(bf16)

    shape = jax.ShapeDtypeStruct((2 * RING * tok, HEAD), bf16)
    return call_on_rows(kernel, "to_blocks", [shape] * heads, core, *chunks, *(tables or ()))


def to_chunks(values, core, tables=None, keyed=False):
    tok = values.shape[0] // (2 * RING)

    def kernel(core_ref, *refs):
        first = core_ref[0] == 0
        for s in range(RING):
            for p in range(2):
                parts = []
                for d, e in ((BACK[s] if p else s, p), (s if p else BACK[s], 1 - p)):
                    place = pl.ds((2 * d + e) * tok, tok)
                    part = refs[0][place, :]
                    if tables is not None:
                        cosine, sine = refs[1][place, :], refs[2][place, :]
                        turned = rotated_halves(part, cosine, -sine)
                        part = jnp.where(first, turned, part) if keyed else turned
                    parts.append(part)
                here = jnp.where(first, parts[0], parts[1])
                refs[-1][pl.ds((2 * s + p) * tok, tok), :] = here.astype(bf16)

    shape = jax.ShapeDtypeStruct(values.shape, bf16)
    return call_on_rows(kernel, "to_chunks", shape, core, values, *(tables or ()))


def mean(values):
    return jnp.mean(values, axis=1, keepdims=True)


def gelu_parts(u):
    k = 0.7978845608028654
    t = jnp.tanh(k * (u + 0.044715 * u * u * u))
    value = 0.5 * u * (1.0 + t)
    slope = 0.5 * (1.0 + t) + 0.5 * u * (1.0 - t * t) * k * (1.0 + 3 * 0.044715 * u * u)
    return value, slope


def body(
    inputs,
    cotangent,
    w_query,
    w_key,
    w_value,
    w_out_t,
    w_gate,
    w_up,
    w_down_t,
    gain_attn_in,
    gain_attn_out,
    gain_mlp_in,
    gain_mlp_out,
):
    tok, width = inputs.shape
    rows = w_query.shape[0]
    count_b, count_y = lax.axis_size("b"), lax.axis_size("y")
    z, b, y, c = [lax.axis_index(name) for name in AXES]

    g_attn = gain_attn_in.astype(f32)[:, None]
    g_mlp = gain_mlp_in.astype(f32)[:, None]

    def scaled(weight, gain):
        return (weight.astype(f32) * gain).astype(bf16)

    pairs = jnp.stack(
        [w_key.reshape(rows, KV_HEADS, HEAD), w_value.reshape(rows, KV_HEADS, HEAD)], axis=2
    ).reshape(rows, 8, HEAD)
    qkv_pack = jnp.concatenate([w_query.reshape(rows, 8, HEAD), pairs], axis=2)
    qkv_pack = (qkv_pack.astype(f32) * g_attn[:, :, None]).astype(bf16)
    qkv_pack = jnp.concatenate([qkv_pack, w_out_t.reshape(rows, 8, HEAD)], axis=2)
    qkv_pack = qkv_pack.transpose(1, 0, 2)
    x, normed_x, r1 = copies_first(inputs, normed=True)
    x = x.astype(f32)
    gate_pack = split_cols(scaled(w_gate, g_mlp))
    up_pack = split_cols(scaled(w_up, g_mlp))
    down_pack = split_cols(w_down_t)
    qkv_w = gather_rows(exchange(qkv_pack))
    qkv_w, out_w = qkv_w[:, : 2 * HEAD], qkv_w[:, 2 * HEAD :]
    gains = jnp.concatenate([gain_attn_out, gain_mlp_out])[None]
    gains = gather_small(gains)
    x1, _, (_, _, (gate_pack,)) = gather_tokens(normed_x, None, (None, None, (gate_pack,)))
    gate_mine = exchange(gate_pack)
    qkv = [dot_nn(part, qkv_w) for part in x1]
    run = 2 * tok

    def starts(places_b, places_y):
        blocks = (z - jnp.arange(RING, dtype=jnp.int32)) % RING
        place = (blocks * count_b + places_b[:, None, None]) * count_y + places_y[:, None]
        return place.reshape(-1) * run

    q_starts = starts(b[None], y[None])
    k_starts = starts(
        (b - jnp.arange(count_b, dtype=jnp.int32)) % count_b,
        (y - jnp.arange(count_y, dtype=jnp.int32)) % count_y,
    )
    meta = jnp.concatenate([c.astype(jnp.int32)[None], q_starts, k_starts])

    core = c.astype(jnp.int32)[None]
    q_pos = (q_starts[:, None] + jnp.arange(run, dtype=jnp.int32)).reshape(-1)
    frequency = 10000.0 ** (-jnp.arange(HEAD // 2, dtype=f32) * 2.0 / HEAD)
    angles = q_pos.astype(f32)[:, None] * frequency[None, :]
    tables = (jnp.cos(angles), jnp.sin(angles))

    q, own_kv = to_blocks(qkv, core, tables)
    kv_mine = jnp.concatenate([moved_on(own_kv, k, j) for k, j in copies_apart()], axis=0)
    kv_mine, gate_mine, up_pack, gains = join(kv_mine, gate_mine, up_pack, gains)
    gate_w = gather_rows(gate_mine)
    up_mine = exchange(up_pack)
    kv_other = swapped(kv_mine, "c")
    attended, lse = attention_forward(q, kv_mine, kv_other, meta, run)
    attended, up_mine, down_pack = join(attended, up_mine, down_pack)
    up_w = gather_rows(up_mine)
    down_mine = exchange(down_pack)
    g_attn_out = moved(gains[:, :rows].reshape(1, width), RING, count_b * count_y)
    g_mlp_out = moved(gains[:, rows:].reshape(1, width), RING, count_b * count_y)
    attended_b = to_chunks(attended, core)
    size = 2 * tok

    def cut(values):
        return [values[i * size : (i + 1) * size] for i in range(RING)]

    projected, ((gate_w,), (down_mine,), _) = scatter_tokens(
        [dot_nt(part, out_w).astype(bf16) for part in cut(attended_b)],
        ((gate_w,), (down_mine,), None),
    )
    down_w = gather_rows(down_mine)
    r2 = lax.rsqrt(mean(projected * projected) + EPS)
    hidden = x + projected * r2 * g_attn_out

    r3 = lax.rsqrt(mean(hidden * hidden) + EPS)
    def mlp_forward(i, part):
        gate = dot_nn(part, gate_w).astype(bf16)
        up = dot_nn(part, up_w).astype(bf16)
        return gate, up, (gelu_parts(gate.astype(f32))[0] * up.astype(f32)).astype(bf16)

    x2, mlp, _ = gather_tokens((hidden * r3).astype(bf16), mlp_forward)
    gate, up, mixed = zip(*mlp)
    *x1, hidden = join(*x1, hidden)
    x1, x2, all_mixed = [jnp.concatenate(parts, axis=0) for parts in (x1, x2, mixed)]
    reduced, ((x2,), (x1, all_mixed), _) = scatter_tokens(
        [dot_nt(part, down_w).astype(bf16) for part in mixed], ((x2,), (x1, all_mixed), None)
    )
    r4 = lax.rsqrt(mean(reduced * reduced) + EPS)

    top = copies_first(cotangent).astype(f32)
    lifted = top * g_mlp_out
    d_reduced = r4 * lifted - reduced * (r4 * r4 * r4 * mean(lifted * reduced))
    def mlp_backward(i, part):
        d_mixed = dot_nn(part, down_w)
        gelu, slope = gelu_parts(gate[i].astype(f32))
        d_gate = (d_mixed * up[i].astype(f32) * slope).astype(bf16)
        d_up = (d_mixed * gelu).astype(bf16)
        return d_gate, d_up, (dot_nt(d_gate, gate_w) + dot_nt(d_up, up_w)).astype(bf16)

    x3, mlp, _ = gather_tokens(d_reduced.astype(bf16), mlp_backward)
    d_gate, d_up, dn3 = zip(*mlp)
    x3 = jnp.concatenate(x3, axis=0)
    down_part = dot_tn(x3, all_mixed).astype(bf16)
    gate_part = dot_tn(x2, jnp.concatenate(d_gate, axis=0)).astype(bf16)
    up_part = dot_tn(x2, jnp.concatenate(d_up, axis=0)).astype(bf16)
    dn3, ((down_part,), (gate_part,), (up_part,)) = scatter_tokens(
        dn3, ((down_part,), (gate_part,), (up_part,))
    )
    down_rows, gate_rows, up_rows = [scatter_rows(p) for p in (down_part, gate_part, up_part)]
    d_hidden = top + r3 * dn3 - hidden * (r3 * r3 * r3 * mean(dn3 * hidden))
    lifted = d_hidden * g_attn_out
    d_projected = r2 * lifted - projected * (r2 * r2 * r2 * mean(lifted * projected))
    d_projected, d_hidden, reduced = join(d_projected.astype(bf16), d_hidden, reduced)
    output = copies_back((hidden + reduced * r4 * g_mlp_out).astype(bf16))
    d_gain_mlp_out = jnp.sum(top * reduced * r4, axis=0, keepdims=True)
    d_gain_attn_out = jnp.sum(d_hidden * projected * r2, axis=0, keepdims=True)
    d_gains = jnp.concatenate(
        [
            moved(d_gain_attn_out, count_b * count_y, RING).reshape(-1, rows),
            moved(d_gain_mlp_out, count_b * count_y, RING).reshape(-1, rows),
        ],
        axis=1,
    )
    d_gains = scatter_small(d_gains)
    x4, d_attended, ((output,), _, _) = gather_tokens(
        d_projected, lambda i, part: (dot_nn(part, out_w).astype(bf16),), ((output,), None, None)
    )
    (d_attended,) = to_blocks([part[0] for part in d_attended], core)
    delta = jnp.sum(d_attended.astype(f32) * attended, axis=1)
    delta, down_rows, gate_rows, d_gains = join(delta, down_rows, gate_rows, d_gains)
    down_sum = exchange(down_rows)
    d_query, d_mine, d_other = attention_backward(
        q, d_attended, kv_mine, kv_other, meta, lse.reshape(1, -1), delta[None], run
    )
    d_query, d_mine, d_other, down_sum, gate_rows = join(
        d_query, d_mine, d_other, down_sum, gate_rows
    )
    gate_sum = exchange(gate_rows)
    d_mine = (d_mine.astype(f32) + swapped(d_other, "c").astype(f32)).astype(bf16)
    d_parts = d_mine.reshape(count_b * count_y, -1, HEAD)
    d_own = sum(
        moved_on(part, k, j, back=True).astype(f32) for part, (k, j) in zip(d_parts, copies_apart())
    )
    d_own, d_query, *x4, gate_sum, up_rows = join(d_own, d_query, *x4, gate_sum, up_rows)
    up_sum = exchange(up_rows)
    d_q = to_chunks(d_query, core, tables)
    d_k = to_chunks(d_own, core, tables, keyed=True)
    d_qkv = jnp.concatenate([d_q, d_k], axis=1)

    def attention_rows(first):
        q_side, k_side, *x4_parts = first
        parts = [
            dot_tn(x1, q_side),
            dot_tn(jnp.concatenate(x4_parts, axis=0), attended_b),
            dot_tn(x1, k_side),
        ]
        return up_sum, scatter_rows(jnp.concatenate(parts, axis=1).astype(bf16))

    dn1, (_, (up_sum, _), (attn_sum,)) = scatter_tokens(
        [dot_nt(part, qkv_w).astype(bf16) for part in cut(d_qkv)],
        (None, attention_rows, lambda before: (exchange(before[1]),)),
        (d_q, d_k, *x4),
    )
    down_sum, gate_sum, up_sum, attn_sum = [
        part.astype(f32) for part in (down_sum, gate_sum, up_sum, attn_sum)
    ]
    q_sum, out_sum, kv_sum = [attn_sum[:, :, i * HEAD : (i + 1) * HEAD] for i in range(3)]
    q_sum, out_sum = join_cols(q_sum), join_cols(out_sum)
    kv_sum = kv_sum.reshape(KV_HEADS, 2, rows, HEAD)
    d_source = r1 * dn1 - x * (r1 * r1 * r1 * mean(dn1 * x))
    input_grad = copies_back((d_hidden + d_source).astype(bf16))

    k_sum, v_sum = join_cols(kv_sum[:, 0]), join_cols(kv_sum[:, 1])
    gate_sum, up_sum = join_cols(gate_sum), join_cols(up_sum)

    def row_term(weight, grad):
        return jnp.sum(weight.astype(f32) * grad, axis=1)

    d_gain_attn_in = (
        row_term(w_query, q_sum) + row_term(w_key, k_sum) + row_term(w_value, v_sum)
    )
    d_gain_mlp_in = row_term(w_gate, gate_sum) + row_term(w_up, up_sum)
    return (
        output,
        input_grad,
        q_sum * g_attn,
        k_sum * g_attn,
        v_sum * g_attn,
        out_sum,
        gate_sum * g_mlp,
        up_sum * g_mlp,
        join_cols(down_sum),
        d_gain_attn_in,
        d_gains[:rows],
        d_gain_mlp_in,
        d_gains[rows:],
    )


def solution(mesh):
    ctx, fsdp = mesh.devices.shape
    laid = Mesh(mesh.devices.reshape(RING, ctx // RING, fsdp // 2, 2), AXES)
    rows = P(AXES, None)
    line = P(AXES)
    return jax.shard_map(
        body,
        mesh=laid,
        in_specs=(rows,) * 9 + (line,) * 4,
        out_specs=(rows,) * 9 + (line,) * 4,
        check_vma=False,
    )
```
